256 devices in a mesh: feat: 64 (over y, z, core), ex: 4 (over x).
Axes of the slice: x: 4, y: 4, z: 8, core: 2. Of those that a mesh axis runs over, the one named last changes fastest.
Arguments:
- examples: bfloat16 [4096, 262144], P('ex', 'feat'), may hold values from -6 to 6
- weights: bfloat16 [262144], P('feat'), may hold values from -0.01171875 to 0.01171875
- labels: int32 [4096], P('ex'), may hold values from 0 to 1
- split: int32 [4096], P('ex'), may hold values 0 or 1
- val_weight: float32 [32, 4096], P(None, 'ex'), may hold values from 0.1 to 10
- strengths: float32 [256], replicated, may hold values from 0.05 to 1
- block_ids: int32 [262144], P('feat'), may hold values from 0 to 255
Outputs:
- solve: float32 [32, 262144], P(None, ('feat', 'ex'))
- hypergrad: float32 [32, 256], P(None, ('feat', 'ex'))
The draws below stay inside these ranges and needn't reach their ends.
All inputs are finite; a program needn't handle non-finite values. No bound on the sum of `split` on one device may be relied on, other than what follows from the above.
Results may differ from the reference program's by a relative error of at most 0.0029.
Values may be sent and summed in bfloat16 or wider, within the bound.
No kernel may reach another device: no remote copies, remote signals or barrier semaphores. Data moves between devices by JAX's collectives and lax.ppermute only.
A program may use at most 64 MiB of HBM per device.

```python
import math
import jax
import jax.numpy as jnp
from jax import lax

F = 262144
NB = 256
R = 32
NEX = 4096


def set_ends(drawn, rng, smallest, high):
    longest = drawn.shape.index(max(drawn.shape))
    spots = []
    for shift in (0, 1):
        where = [jax.random.randint(jax.random.fold_in(rng, axis), (), 0, length) for axis, length in enumerate(drawn.shape)]
        where[longest] = (where[longest] + shift) % drawn.shape[longest]
        spots.append(tuple(where))
    return drawn.at[spots[0]].set(smallest).at[spots[1]].set(high)


def block_levels(key, shape, cuts, least, largest):
    def one(position, blocks):
        draws = jax.random.uniform(jax.random.fold_in(jax.random.fold_in(key, 6), position), (blocks,), jnp.float32, least / len(cuts), largest / len(cuts))
        return jnp.repeat(jnp.exp(draws), shape[position] // blocks).reshape((-1,) + (1,) * (len(shape) - position - 1))

    gain = one(*cuts[0])
    for cut in cuts[1:]:
        gain = gain * one(*cut)
    return gain


def gaussian(key, extent, scale, reach, shards=(), kind=jnp.bfloat16):
    array = scale * jax.random.normal(key, extent, jnp.float32)
    if shards:
        array = array * block_levels(key, extent, shards, -0.22, 0.18)
    return jnp.clip(array, -reach, reach).astype(kind)


def setup_inputs(seed: int = 0) -> dict:
    seeds = jax.random.split(jax.random.key(seed), 8)
    examples = gaussian(seeds[0], (NEX, F), 1.0, 6.0, ((0, 4), (1, 64)))
    weights = gaussian(seeds[1], (F,), F ** -0.5, 0.01171875, ((0, 64),))
    labels = set_ends(jax.random.randint(seeds[2], (NEX,), 0, 2), jax.random.fold_in(seeds[2], 1), 0, 1).astype(jnp.int32)
    split = set_ends((jax.random.randint(seeds[3], (NEX,), 0, 4) < 3).astype(jnp.int32), jax.random.fold_in(seeds[3], 1), 0, 1)
    val_weight = jnp.clip(jnp.exp(math.log(10.0) - 4.6051702 * jax.random.uniform(seeds[4], (R, NEX), jnp.float32) ** block_levels(seeds[4], (R, NEX), ((1, 4),), -0.2, 0.2)), 0.1, 10.0)
    strengths = jnp.clip(jnp.exp(jax.random.uniform(seeds[5], (NB,), jnp.float32, math.log(0.05), math.log(1.0))), 0.05, 1.0)
    block_ids = set_ends(jax.random.randint(seeds[6], (F,), 0, NB), jax.random.fold_in(seeds[6], 1), 0, NB - 1).astype(jnp.int32)
    return {"examples": examples, "weights": weights, "labels": labels, "split": split, "val_weight": val_weight, "strengths": strengths, "block_ids": block_ids}


def reference(examples, weights, labels, split, val_weight, strengths, block_ids):
    margin = jnp.dot(examples, weights, preferred_element_type=jnp.float32)
    prob = 1.0 / (1.0 + jnp.exp(-margin))
    train = split.astype(jnp.float32)
    curvew = train * prob * (1.0 - prob)
    err = (1.0 - train) * (prob - labels.astype(jnp.float32))
    gradw = (val_weight * err[None, :] / jnp.sqrt(jnp.float32(NEX))).astype(jnp.bfloat16)
    rhs = jnp.dot(gradw, examples, preferred_element_type=jnp.float32)
    lamf = strengths[block_ids]

    def apply_hessian(direc):
        dlow = direc.astype(jnp.bfloat16)
        tang = jnp.dot(dlow, examples.T, preferred_element_type=jnp.float32)
        wtang = (curvew[None, :] * tang).astype(jnp.bfloat16)
        prod = jnp.dot(wtang, examples, preferred_element_type=jnp.float32)
        return prod / jnp.float32(NEX) + lamf[None, :] * direc
    solve = jnp.zeros_like(rhs)
    resid = rhs
    direc = rhs
    norm_now = lax.optimization_barrier(jnp.sum(resid * resid, axis=1))
    for step in range(2):
        image = apply_hessian(direc)
        curv = lax.optimization_barrier(jnp.sum(direc * image, axis=1))
        alpha = norm_now / curv
        solve = solve + alpha[:, None] * direc
        resid = resid - alpha[:, None] * image
        if step == 0:
            norm_next = lax.optimization_barrier(jnp.sum(resid * resid, axis=1))
            direc = resid + (norm_next / norm_now)[:, None] * direc
            norm_now = norm_next
    product = solve * weights.astype(jnp.float32)[None, :]
    sums = jax.ops.segment_sum(product.T, block_ids, num_segments=NB).T
    return (solve, -strengths[None, :] * sums)
```

```python
import functools

import jax
import jax.numpy as jnp
from jax import lax
from jax.experimental import pallas as pl
from jax.experimental.pallas import tpu as pltpu
from jax.sharding import Mesh
from jax.sharding import PartitionSpec as P

F32 = jnp.float32
BF16 = jnp.bfloat16
NT = (((1,), (1,)), ((), ()))
NY, NZ, NC, NX = 4, 8, 2, 4
R = 32
N = 1024
HALF = N // NC
W = 4096
OWN = W // NX
NB = 256
TOTAL = float(N * NX)
LANES = 128
VMEM = pl.BlockSpec(memory_space=pltpu.VMEM)
SMEM = pl.BlockSpec(memory_space=pltpu.SMEM)


def call(body, outs, *arrays, scratch=(), limit=16, smem=()):
    return pl.pallas_call(
        body,
        out_shape=outs,
        in_specs=[SMEM if i in smem else VMEM for i in range(len(arrays))],
        out_specs=jax.tree.map(lambda _: VMEM, outs),
        scratch_shapes=scratch,
        compiler_params=pltpu.CompilerParams(vmem_limit_bytes=limit << 20),
    )(*arrays)


def shape(*dims, dtype=F32):
    return jax.ShapeDtypeStruct(dims, dtype)


def lane_ids(lanes=LANES):
    return lax.broadcasted_iota(jnp.int32, (R, lanes), 1)


def column(tile, lane):
    return jnp.sum(jnp.where(lane_ids(tile.shape[1]) == lane, tile, 0.0), axis=1, keepdims=True)


def columns(values, first=0):
    lanes = lane_ids()
    tile = jnp.zeros((R, LANES), F32)
    for i, value in enumerate(values):
        tile = jnp.where(lanes == first + i, value, tile)
    return tile


def terms(value, count):
    found = []
    for _ in range(count):
        term = value.astype(BF16).astype(F32)
        found.append(term)
        value = value - term
    return found


def packed(values):
    return columns([term for value in values for term in terms(value, 3)])


def unpacked(tile, index):
    lanes = lane_ids()
    inside = (lanes >= 3 * index) & (lanes < 3 * index + 3)
    return jnp.sum(jnp.where(inside, tile, 0.0), axis=1, keepdims=True)


def chunk(index, size):
    return pl.ds(pl.multiple_of(index * size, size), size)


def block_sums(vec, weight, onehot):
    parts = jnp.concatenate(terms(vec * weight, 3), axis=0).astype(BF16)
    sums = lax.dot_general(parts, onehot, NT, preferred_element_type=F32)
    return sums[:R] + sums[R : 2 * R] + sums[2 * R :]


def prepare(ids, strengths, place, lamf, onehot):
    kinds = lax.broadcasted_iota(jnp.int32, (NB, OWN), 0)
    rows = lax.broadcasted_iota(jnp.int32, (16, NB), 0)
    value = strengths[...]
    split3 = jnp.zeros((16, NB), F32)
    for i, term in enumerate(terms(value, 3)):
        split3 = jnp.where(rows == i, term, split3)
    split3 = split3.astype(BF16)
    for j in range(NX):
        hot = (kinds == ids[:, j * OWN : (j + 1) * OWN]).astype(F32).astype(BF16)
        found = jnp.dot(split3, hot, preferred_element_type=F32)
        lamf[:, j * OWN : (j + 1) * OWN] = found[0:1] + found[1:2] + found[2:3]
    own = ids[:, chunk(place[3], OWN)]
    core = lax.shift_right_logical(own, 2) & 1
    moved = core * 128 + lax.shift_right_logical(own, 3) * 4 + (own & 3)
    onehot[...] = (kinds == moved).astype(F32).astype(BF16)


def margins(examples, weights, margin):
    for i in range(8):
        rows = lax.dot_general(
            weights[...], examples[i * 128 : (i + 1) * 128, :], NT, preferred_element_type=F32
        )
        margin[i : i + 1, :] = rows[0:1]


def gradients(margin_parts, labels, split, val_weight, examples, part, curvew):
    whole = jnp.sum(margin_parts[...], axis=0)
    margin = jnp.concatenate([whole[i : i + 1] for i in range(8)], axis=1)
    prob = 1.0 / (1.0 + jnp.exp(-margin))
    train = split[...].astype(F32)
    curvew[...] = train * prob * (1.0 - prob)
    err = (1.0 - train) * (prob - labels[...].astype(F32))
    gradw = (val_weight[...] * err / jnp.sqrt(F32(TOTAL))).astype(BF16)
    for j in range(NX):

        def step(i, _, j=j):
            at = chunk(i, 256)
            cols = pl.ds(pl.multiple_of(j * OWN + i * 256, 256), 256)
            part[j, :, at] = jnp.dot(gradw, examples[:, cols], preferred_element_type=F32)
            return 0

        lax.fori_loop(0, OWN // 256, step, 0)


def start_rhs(arrived, rhs, low):
    total = jnp.sum(arrived[...], axis=0)
    rhs[...] = total
    low[...] = total.astype(BF16)


def rhs_sums(rhs, lamf, wfloat, onehot, place, sums):
    own = chunk(place[3], OWN)
    vec = rhs[...]
    norm = jnp.sum(vec * vec, axis=1, keepdims=True)
    scaled = jnp.sum(lamf[:, own] * vec * vec, axis=1, keepdims=True)
    sums[:, :LANES] = columns([norm, scaled])
    sums[:, LANES:] = block_sums(vec, wfloat[:, own], onehot[...])


def tangents(pieces, examples, x, tang):
    def step(i, _):
        rows = chunk(i, 256)
        total = None
        for s, piece in enumerate(pieces):
            cols = chunk((x - s + NX) % NX, OWN)
            term = lax.dot_general(
                piece[...], examples[rows, cols], NT, preferred_element_type=F32
            )
            total = term if total is None else total + term
        tang[:, rows] = total
        return 0

    lax.fori_loop(0, N // 256, step, 0)


def halves(tang, scalars, blocks, core, keep, send):
    for out, which in ((keep, core), (send, 1 - core)):
        out[:, :HALF] = tang[:, chunk(which, HALF)]
        out[:, HALF : HALF + LANES] = scalars
        out[:, HALF + LANES :] = blocks[:, chunk(which, LANES)]


def first_tangents(low0, low1, low2, low3, examples, sums, place, keep, send, tang, blocks):
    tangents([low0, low1, low2, low3], examples, place[3], tang)
    blocks[...] = sums[:, LANES:]
    halves(tang, sums[:, :LANES], blocks, place[2], keep, send)


def to_wire(keep, arrived, wire):
    total = keep[...] + arrived[...]
    wire[:, :HALF] = total[:, :HALF].astype(BF16)
    scalars = total[:, HALF : HALF + LANES]
    wire[:, HALF : HALF + LANES] = packed([column(scalars, i) for i in range(3)]).astype(BF16)
    high, rest = terms(total[:, HALF + LANES :], 2)
    wire[:, HALF + LANES : HALF + 2 * LANES] = high.astype(BF16)
    wire[:, HALF + 2 * LANES :] = rest.astype(BF16)


def along_y(wire0, wire1, wire2, wire3, place, out):
    total = wire0[...].astype(F32)
    for wire in (wire1, wire2, wire3):
        total = total + wire[...].astype(F32)
    tang = total[:, :HALF].astype(BF16)
    scalars = total[:, HALF : HALF + LANES]
    tile = packed([unpacked(scalars, i) for i in range(3)])
    blocks = total[:, HALF + LANES : HALF + 2 * LANES] + total[:, HALF + 2 * LANES :]
    lanes = lane_ids()
    at64 = pltpu.roll(blocks, (64 - 32 * place[0] + LANES) % LANES, 1)
    at96 = pltpu.roll(blocks, (96 - 32 * place[0] + LANES) % LANES, 1)
    tile = jnp.where((lanes >= 64) & (lanes < 96), terms(at64, 1)[0], tile)
    tile = jnp.where(lanes >= 96, terms(at96, 2)[1], tile)
    tile = tile.astype(BF16)
    for i in range(NZ):
        out[i, :, :HALF] = tang
        out[i, :, HALF:] = tile


def along_z(arrived):
    tang = arrived[0, :, :HALF].astype(F32)
    tile = arrived[0, :, HALF:].astype(F32)
    for i in range(1, NZ):
        tang = tang + arrived[i, :, :HALF].astype(F32)
        tile = tile + arrived[i, :, HALF:].astype(F32)
    scalars = [unpacked(tile, i) for i in range(3)]
    blocks = pltpu.roll(tile, 64, 1) + pltpu.roll(tile, 32, 1)
    return tang, scalars, jnp.where(lane_ids() < 32, blocks, 0.0)


def weigh(arrived, curvew, place, tang_out, weighted, kept):
    tang, (norm, scaled, _), blocks = along_z(arrived)
    tang_out[...] = tang
    half = curvew[:, chunk(place[2], HALF)]
    product = half * tang
    curv = jnp.sum(product * tang, axis=1, keepdims=True)
    weighted[:, :HALF] = product.astype(BF16)
    weighted[:, HALF:] = packed([curv]).astype(BF16)
    kept[:, :LANES] = columns([norm, scaled, curv])
    kept[:, LANES:] = blocks


def products(weighted, other, kept, examples, place, part):
    core = place[2]

    def step(i, _):
        cols = chunk(i, 256)
        mine = jnp.dot(
            weighted[:, :HALF], examples[chunk(core, HALF), cols], preferred_element_type=F32
        )
        rest = jnp.dot(
            other[:, :HALF], examples[chunk(1 - core, HALF), cols], preferred_element_type=F32
        )
        part[:, cols] = (mine + rest).astype(BF16)
        return 0

    lax.fori_loop(0, W // 256, step, 0)
    tile = kept[:, :LANES]
    curv = column(tile, 2) + unpacked(other[:, HALF:].astype(F32), 0)
    part[:, W:] = packed([column(tile, 0), column(tile, 1), curv]).astype(BF16)


def second_tangents(
    part0, part1, part2, part3, rhs, low1, low2, low3, examples, lamf, wfloat, onehot, place,
    resid, keep, send, kept, tang, blocks, pieces,
):
    x = place[3]
    parts = (part0, part1, part2, part3)
    tile = sum(p[:, W:].astype(F32) for p in parts)
    norm, scaled, curv = (unpacked(tile, i) for i in range(3))
    alpha = norm / (curv / F32(TOTAL) + scaled)
    kept[...] = columns([alpha, norm, scaled, curv])
    for s, vec in enumerate((rhs, low1, low2, low3)):
        cols = chunk((x - s + NX) % NX, OWN)
        total = sum(p[:, cols].astype(F32) for p in parts)
        direc = vec[...].astype(F32)
        lam = lamf[:, cols]
        left = direc - alpha * (total / F32(TOTAL) + lam * direc)
        pieces[s] = left.astype(BF16)
        if s == 0:
            resid[...] = left
            scalars = columns(
                [
                    jnp.sum(left * left, axis=1, keepdims=True),
                    jnp.sum(lam * left * left, axis=1, keepdims=True),
                    jnp.sum(lam * left * direc, axis=1, keepdims=True),
                ]
            )
            blocks[...] = block_sums(left, wfloat[:, cols], onehot[...])
    tangents([pieces.at[s] for s in range(NX)], examples, x, tang)
    halves(tang, scalars, blocks, place[2], keep, send)


def curvature(arrived, curvew, tang_first, kept, place, out):
    tang, (norm, scaled, mixed), blocks = along_z(arrived)
    half = curvew[:, chunk(place[2], HALF)]
    product = half * tang
    both = jnp.sum(product * tang, axis=1, keepdims=True)
    cross = jnp.sum(product * tang_first[...], axis=1, keepdims=True)
    tile = columns([both, cross, norm, scaled, mixed])
    lanes = lane_ids()
    shift = 4 * place[1]
    now = pltpu.roll(blocks, (32 - shift + LANES) % LANES, 1)
    before = pltpu.roll(kept[:, LANES:], (36 - shift + LANES) % LANES, 1)
    tile = jnp.where((lanes >= 32) & (lanes < 36), now, tile)
    tile = jnp.where((lanes >= 36) & (lanes < 40), before, tile)
    for i in range(NC * NX):
        out[i] = tile


def finish(arrived, kept, rhs, resid, strengths, place, solve, hyper):
    core, x = place[2], place[3]
    mine = sum(arrived[core * NX + i] for i in range(NX))
    rest = sum(arrived[(1 - core) * NX + i] for i in range(NX))
    every = mine + rest
    tile = kept[...]
    alpha, norm, scaled_first, curv_first = (column(tile, i) for i in range(4))
    both, cross = column(every, 0), column(every, 1)
    norm_next, scaled, mixed = (column(mine, i) for i in range(2, 5))
    beta = norm_next / norm
    curv = (both + 2.0 * beta * cross + beta * beta * curv_first) / F32(TOTAL)
    curv = curv + (scaled + 2.0 * beta * mixed + beta * beta * scaled_first)
    alpha_next = norm_next / curv
    first = rhs[...]
    solve[...] = alpha * first + alpha_next * (resid[...] + beta * first)
    now, before = column(mine, 32 + x), column(mine, 36 + x)
    block = ((place[0] * NZ + place[1]) * NC + core) * NX + x
    kinds = lax.broadcasted_iota(jnp.int32, (1, NB), 1)
    strength = jnp.sum(jnp.where(kinds == block, strengths[...], 0.0), axis=1, keepdims=True)
    hyper[...] = -strength * (alpha * before + alpha_next * (now + beta * before))


def shifted(array, axis, length):
    return [
        lax.ppermute(array, axis, [(i, (i + s) % length) for i in range(length)])
        for s in range(1, length)
    ]


def swapped(array):
    return lax.ppermute(array, "c", [(0, 1), (1, 0)])


def summed(keep, send, place):
    wire = call(to_wire, shape(R, HALF + 3 * LANES, dtype=BF16), keep, swapped(send))
    arrived = shifted(wire, "y", NY)
    out = call(
        along_y, shape(NZ, R, HALF + LANES, dtype=BF16), wire, *arrived, place, smem=(4,)
    )
    return lax.all_to_all(out, "z", 0, 0, tiled=True)


def shards(examples, weights, labels, split, val_weight, strengths, block_ids):
    place = jnp.stack([lax.axis_index(axis) for axis in ("y", "z", "c", "x")]).astype(jnp.int32)
    ids = block_ids.reshape(1, W)
    strengths = strengths.reshape(1, NB)
    wrows = jnp.broadcast_to(weights[None, :], (16, W))
    wfloat = weights.astype(F32).reshape(1, W)
    lamf, onehot = call(
        prepare, [shape(1, W), shape(NB, OWN, dtype=BF16)], ids, strengths, place, smem=(2,)
    )
    margin = call(margins, shape(8, 128), examples, wrows)
    margin = margin + swapped(margin)
    margin_parts = lax.all_to_all(
        jnp.broadcast_to(margin[None], (NY * NZ, 8, 128)), ("y", "z"), 0, 0, tiled=True
    )
    part, curvew = call(
        gradients,
        [shape(NX, R, OWN), shape(1, N)],
        margin_parts,
        labels.reshape(1, N),
        split.reshape(1, N),
        val_weight,
        examples,
    )
    arrived = lax.all_to_all(part, "x", 0, 0, tiled=True)
    rhs, low = call(start_rhs, [shape(R, OWN), shape(R, OWN, dtype=BF16)], arrived)
    lows = shifted(low, "x", NX)
    sums = call(rhs_sums, shape(R, LANES + NB), rhs, lamf, wfloat, onehot, place, smem=(4,))
    pair = [shape(R, HALF + 2 * LANES)] * 2
    keep, send = call(
        first_tangents,
        pair,
        low,
        *lows,
        examples,
        sums,
        place,
        scratch=[pltpu.VMEM((R, N), F32), pltpu.VMEM((R, NB), F32)],
        smem=(6,),
    )
    arrived = summed(keep, send, place)
    tang_first, weighted, kept_first = call(
        weigh,
        [shape(R, HALF), shape(R, HALF + LANES, dtype=BF16), shape(R, 2 * LANES)],
        arrived,
        curvew,
        place,
        smem=(2,),
    )
    part = call(
        products,
        shape(R, W + LANES, dtype=BF16),
        weighted,
        swapped(weighted),
        kept_first,
        examples,
        place,
        smem=(4,),
    )
    resid, keep, send, kept = call(
        second_tangents,
        [shape(R, OWN), *pair, shape(R, LANES)],
        part,
        *shifted(part, "x", NX),
        rhs,
        *lows,
        examples,
        lamf,
        wfloat,
        onehot,
        place,
        scratch=[
            pltpu.VMEM((R, N), F32),
            pltpu.VMEM((R, NB), F32),
            pltpu.VMEM((NX, R, OWN), BF16),
        ],
        smem=(12,),
    )
    arrived = summed(keep, send, place)
    out = call(
        curvature,
        shape(NC * NX, R, LANES),
        arrived,
        curvew,
        tang_first,
        kept_first,
        place,
        smem=(4,),
    )
    arrived = lax.all_to_all(out, ("c", "x"), 0, 0, tiled=True)
    return tuple(
        call(
            finish,
            [shape(R, OWN), shape(R, 1)],
            arrived,
            kept,
            rhs,
            resid,
            strengths,
            place,
            smem=(5,),
        )
    )


def solution(mesh):
    fine = Mesh(mesh.devices.reshape(NY, NZ, NC, NX), ("y", "z", "c", "x"))
    feat = ("y", "z", "c")
    placed = (P("x", feat), P(feat), P("x"), P("x"), P(None, "x"), P(), P(feat))
    return jax.shard_map(
        shards,
        mesh=fine,
        in_specs=placed,
        out_specs=(P(None, (*feat, "x")), P(None, (*feat, "x"))),
        check_vma=False,
    )
```

```python
import jax
import jax.numpy as jnp
from jax import lax
from jax.experimental import pallas as pl
from jax.experimental.pallas import tpu as pltpu
from jax.sharding import Mesh
from jax.sharding import PartitionSpec as P

F32 = jnp.float32
BF16 = jnp.bfloat16
NT = (((1,), (1,)), ((), ()))
NY, NZ, NC, NX = 4, 8, 2, 4
R = 32
N = 1024
HALF = N // NC
W = 4096
OWN = W // NX
NB = 256
TOTAL = float(N * NX)
LANES = 128
VMEM = pl.BlockSpec(memory_space=pltpu.VMEM)
SMEM = pl.BlockSpec(memory_space=pltpu.SMEM)


def call(body, outs, *arrays, scratch=(), limit=16, smem=()):
    return pl.pallas_call(
        body,
        out_shape=outs,
        in_specs=[SMEM if i in smem else VMEM for i in range(len(arrays))],
        out_specs=jax.tree.map(lambda _: VMEM, outs),
        scratch_shapes=scratch,
        compiler_params=pltpu.CompilerParams(vmem_limit_bytes=limit << 20),
    )(*arrays)


def shape(*dims, dtype=F32):
    return jax.ShapeDtypeStruct(dims, dtype)


def lane_ids(lanes=LANES):
    return lax.broadcasted_iota(jnp.int32, (R, lanes), 1)


def column(tile, lane):
    return jnp.sum(jnp.where(lane_ids(tile.shape[1]) == lane, tile, 0.0), axis=1, keepdims=True)


def columns(values, first=0):
    lanes = lane_ids()
    tile = jnp.zeros((R, LANES), F32)
    for i, value in enumerate(values):
        tile = jnp.where(lanes == first + i, value, tile)
    return tile


def terms(value, count):
    found = []
    for _ in range(count):
        term = value.astype(BF16).astype(F32)
        found.append(term)
        value = value - term
    return found


def packed(values):
    return columns([term for value in values for term in terms(value, 3)])


def unpacked(tile, index):
    lanes = lane_ids()
    inside = (lanes >= 3 * index) & (lanes < 3 * index + 3)
    return jnp.sum(jnp.where(inside, tile, 0.0), axis=1, keepdims=True)


def chunk(index, size):
    return pl.ds(pl.multiple_of(index * size, size), size)


def block_sums(vec, weight, onehot):
    parts = jnp.concatenate(terms(vec * weight, 3), axis=0).astype(BF16)
    sums = lax.dot_general(parts, onehot, NT, preferred_element_type=F32)
    return sums[:R] + sums[R : 2 * R] + sums[2 * R :]


def prepare(ids, strengths, place, lamf, onehot):
    kinds = lax.broadcasted_iota(jnp.int32, (NB, OWN), 0)
    rows = lax.broadcasted_iota(jnp.int32, (16, NB), 0)
    split3 = jnp.zeros((16, NB), F32)
    for i, term in enumerate(terms(strengths[...], 3)):
        split3 = jnp.where(rows == i, term, split3)
    split3 = split3.astype(BF16)
    for j in range(NX):
        hot = (kinds == ids[:, j * OWN : (j + 1) * OWN]).astype(F32).astype(BF16)
        found = jnp.dot(split3, hot, preferred_element_type=F32)
        lamf[:, j * OWN : (j + 1) * OWN] = found[0:1] + found[1:2] + found[2:3]
    own = ids[:, chunk(place[3], OWN)]
    core = lax.shift_right_logical(own, 2) & 1
    moved = core * 128 + lax.shift_right_logical(own, 3) * 4 + (own & 3)
    onehot[...] = (kinds == moved).astype(F32).astype(BF16)


def margins(
    source, wfloat, ids, strengths, place, margin, examples, lamf, onehot, arrival
):
    def fetch(i):
        rows = pl.ds(i * 128, 128)
        return pltpu.make_async_copy(source.at[rows], examples.at[rows], arrival.at[i])

    for i in range(8):
        fetch(i).start()
    prepare(ids, strengths, place, lamf, onehot)
    weights = jnp.broadcast_to(wfloat[...], (16, W)).astype(BF16)
    for i in range(8):
        fetch(i).wait()
        rows = lax.dot_general(
            weights, examples[i * 128 : (i + 1) * 128, :], NT, preferred_element_type=F32
        )
        margin[i : i + 1, :] = rows[0:1]


def gradients(
    margin_parts, labels, split, val_weight, examples, place, part, send1, send2, send3, curvew
):
    whole = jnp.sum(margin_parts[...], axis=0)
    margin = jnp.concatenate([whole[i : i + 1] for i in range(8)], axis=1)
    prob = 1.0 / (1.0 + jnp.exp(-margin))
    train = split[...].astype(F32)
    curvew[...] = train * prob * (1.0 - prob)
    err = (1.0 - train) * (prob - labels[...].astype(F32))
    gradw = (val_weight[...] * err / jnp.sqrt(F32(TOTAL))).astype(BF16)
    sends = (send1, send2, send3)
    for j in range(W // 512):
        cols = slice(j * 512, (j + 1) * 512)
        found = jnp.dot(gradw, examples[:, cols], preferred_element_type=F32)
        part[:, cols] = found
        high = found.astype(BF16)
        for send in sends:
            send[:, cols] = high
    for s, send in enumerate(sends):
        found = part[:, chunk((place[3] + s + 1) % NX, OWN)]
        send[:, W:] = (found - found.astype(BF16).astype(F32)).astype(BF16)


def tangents(pieces, examples, x, tang):
    for i in range(N // 256):
        rows = slice(i * 256, (i + 1) * 256)
        total = None
        for s, piece in enumerate(pieces):
            cols = chunk((x - s + NX) % NX, OWN)
            term = lax.dot_general(
                piece[...], examples[rows, cols], NT, preferred_element_type=F32
            )
            total = term if total is None else total + term
        tang[:, rows] = total


def halves(tang, scalars, blocks, core, keep, send):
    for out, which in ((keep, core), (send, 1 - core)):
        out[:, :HALF] = tang[:, chunk(which, HALF)]
        out[:, HALF : HALF + LANES] = scalars
        out[:, HALF + LANES :] = blocks[:, chunk(which, LANES)]


def first_tangents(
    part, wire1, wire2, wire3, examples, lamf, wfloat, onehot, place,
    rhs, lows, keep, send, tang, blocks,
):
    x = place[3]
    wires = (wire1, wire2, wire3)
    for s in range(NX):
        cols = chunk((x - s + NX) % NX, OWN)
        vec = part[:, cols] + sum(w[:, cols].astype(F32) for w in wires)
        if s == 0:
            vec = vec + sum(w[:, W:].astype(F32) for w in wires)
            rhs[...] = vec
            square = vec * vec
            norm = jnp.sum(square, axis=1, keepdims=True)
            scaled = jnp.sum(lamf[:, cols] * square, axis=1, keepdims=True)
            blocks[...] = block_sums(vec, wfloat[:, cols], onehot[...])
        lows[s] = vec.astype(BF16)
    tangents([lows.at[s] for s in range(NX)], examples, x, tang)
    halves(tang, columns([norm, scaled]), blocks, place[2], keep, send)


def to_wire(keep, arrived, wire):
    total = keep[...] + arrived[...]
    wire[:, :HALF] = total[:, :HALF].astype(BF16)
    scalars = total[:, HALF : HALF + LANES]
    wire[:, HALF : HALF + LANES] = packed([column(scalars, i) for i in range(3)]).astype(BF16)
    high, rest = terms(total[:, HALF + LANES :], 2)
    wire[:, HALF + LANES : HALF + 2 * LANES] = high.astype(BF16)
    wire[:, HALF + 2 * LANES :] = rest.astype(BF16)


def along_y(wire0, wire1, wire2, wire3, place, out):
    total = wire0[...].astype(F32)
    for wire in (wire1, wire2, wire3):
        total = total + wire[...].astype(F32)
    tang = total[:, :HALF].astype(BF16)
    scalars = total[:, HALF : HALF + LANES]
    tile = packed([unpacked(scalars, i) for i in range(3)])
    blocks = total[:, HALF + LANES : HALF + 2 * LANES] + total[:, HALF + 2 * LANES :]
    lanes = lane_ids()
    at64 = pltpu.roll(blocks, (64 - 32 * place[0] + LANES) % LANES, 1)
    at96 = pltpu.roll(blocks, (96 - 32 * place[0] + LANES) % LANES, 1)
    tile = jnp.where((lanes >= 64) & (lanes < 96), terms(at64, 1)[0], tile)
    tile = jnp.where(lanes >= 96, terms(at96, 2)[1], tile)
    tile = tile.astype(BF16)
    for i in range(NZ):
        out[i, :, :HALF] = tang
        out[i, :, HALF:] = tile


def along_z(arrived):
    tang = arrived[0, :, :HALF].astype(F32)
    tile = arrived[0, :, HALF:].astype(F32)
    for i in range(1, NZ):
        tang = tang + arrived[i, :, :HALF].astype(F32)
        tile = tile + arrived[i, :, HALF:].astype(F32)
    scalars = [unpacked(tile, i) for i in range(3)]
    blocks = pltpu.roll(tile, 64, 1) + pltpu.roll(tile, 32, 1)
    return tang, scalars, jnp.where(lane_ids() < 32, blocks, 0.0)


def weigh(arrived, curvew, place, tang_out, weighted, kept):
    tang, (norm, scaled, _), blocks = along_z(arrived)
    tang_out[...] = tang
    half = curvew[:, chunk(place[2], HALF)]
    product = half * tang
    curv = jnp.sum(product * tang, axis=1, keepdims=True)
    weighted[:, :HALF] = product.astype(BF16)
    weighted[:, HALF:] = packed([curv]).astype(BF16)
    kept[:, :LANES] = columns([norm, scaled, curv])
    kept[:, LANES:] = blocks


def products(weighted, other, kept, examples, place, part):
    core = place[2]
    for j in range(W // 512):
        cols = slice(j * 512, (j + 1) * 512)
        mine = jnp.dot(
            weighted[:, :HALF], examples[chunk(core, HALF), cols], preferred_element_type=F32
        )
        rest = jnp.dot(
            other[:, :HALF], examples[chunk(1 - core, HALF), cols], preferred_element_type=F32
        )
        part[:, cols] = (mine + rest).astype(BF16)
    tile = kept[:, :LANES]
    curv = column(tile, 2) + unpacked(other[:, HALF:].astype(F32), 0)
    part[:, W:] = packed([column(tile, 0), column(tile, 1), curv]).astype(BF16)


def second_tangents(
    part0, part1, part2, part3, rhs, lows, examples, lamf, wfloat, onehot, place,
    resid, keep, send, kept, tang, blocks, pieces,
):
    x = place[3]
    parts = (part0, part1, part2, part3)
    tile = sum(p[:, W:].astype(F32) for p in parts)
    norm, scaled, curv = (unpacked(tile, i) for i in range(3))
    alpha = norm / (curv / F32(TOTAL) + scaled)
    kept[...] = columns([alpha, norm, scaled, curv])
    for s in range(NX):
        cols = chunk((x - s + NX) % NX, OWN)
        total = sum(p[:, cols].astype(F32) for p in parts)
        direc = rhs[...] if s == 0 else lows[s].astype(F32)
        lam = lamf[:, cols]
        left = direc - alpha * (total / F32(TOTAL) + lam * direc)
        pieces[s] = left.astype(BF16)
        if s == 0:
            resid[...] = left
            scalars = columns(
                [
                    jnp.sum(left * left, axis=1, keepdims=True),
                    jnp.sum(lam * left * left, axis=1, keepdims=True),
                    jnp.sum(lam * left * direc, axis=1, keepdims=True),
                ]
            )
            blocks[...] = block_sums(left, wfloat[:, cols], onehot[...])
    tangents([pieces.at[s] for s in range(NX)], examples, x, tang)
    halves(tang, scalars, blocks, place[2], keep, send)


def curvature(arrived, curvew, tang_first, kept, place, out):
    tang, (norm, scaled, mixed), blocks = along_z(arrived)
    half = curvew[:, chunk(place[2], HALF)]
    product = half * tang
    both = jnp.sum(product * tang, axis=1, keepdims=True)
    cross = jnp.sum(product * tang_first[...], axis=1, keepdims=True)
    tile = columns([both, cross, norm, scaled, mixed])
    lanes = lane_ids()
    shift = 4 * place[1]
    now = pltpu.roll(blocks, (32 - shift + LANES) % LANES, 1)
    before = pltpu.roll(kept[:, LANES:], (36 - shift + LANES) % LANES, 1)
    tile = jnp.where((lanes >= 32) & (lanes < 36), now, tile)
    tile = jnp.where((lanes >= 36) & (lanes < 40), before, tile)
    for i in range(NC * NX):
        out[i] = tile


def finish(arrived, kept, rhs, resid, strengths, place, solve, hyper):
    core, x = place[2], place[3]
    mine = sum(arrived[core * NX + i] for i in range(NX))
    rest = sum(arrived[(1 - core) * NX + i] for i in range(NX))
    every = mine + rest
    tile = kept[...]
    alpha, norm, scaled_first, curv_first = (column(tile, i) for i in range(4))
    both, cross = column(every, 0), column(every, 1)
    norm_next, scaled, mixed = (column(mine, i) for i in range(2, 5))
    beta = norm_next / norm
    curv = (both + 2.0 * beta * cross + beta * beta * curv_first) / F32(TOTAL)
    curv = curv + (scaled + 2.0 * beta * mixed + beta * beta * scaled_first)
    alpha_next = norm_next / curv
    first = rhs[...]
    solve[...] = alpha * first + alpha_next * (resid[...] + beta * first)
    now, before = column(mine, 32 + x), column(mine, 36 + x)
    block = ((place[0] * NZ + place[1]) * NC + core) * NX + x
    kinds = lax.broadcasted_iota(jnp.int32, (1, NB), 1)
    strength = jnp.sum(jnp.where(kinds == block, strengths[...], 0.0), axis=1, keepdims=True)
    found = -strength * (alpha * before + alpha_next * (now + beta * before))
    hyper[...] = jnp.transpose(jnp.broadcast_to(found, (R, LANES)))[0:1]


def shift(array, axis, length, by):
    return lax.ppermute(array, axis, [(i, (i + by) % length) for i in range(length)])


def shifted(array, axis, length):
    return [shift(array, axis, length, s) for s in range(1, length)]


def swapped(array):
    return lax.ppermute(array, "c", [(0, 1), (1, 0)])


def summed(keep, send, place):
    wire = call(to_wire, shape(R, HALF + 3 * LANES, dtype=BF16), keep, swapped(send))
    arrived = shifted(wire, "y", NY)
    out = call(
        along_y, shape(NZ, R, HALF + LANES, dtype=BF16), wire, *arrived, place, smem=(4,)
    )
    return lax.all_to_all(out, "z", 0, 0, tiled=True)


def shards(examples, weights, labels, split, val_weight, strengths, block_ids):
    place = jnp.stack([lax.axis_index(axis) for axis in ("y", "z", "c", "x")]).astype(jnp.int32)
    strengths = strengths.reshape(1, NB)
    wfloat = weights.astype(F32).reshape(1, W)
    margin, examples, lamf, onehot = pl.pallas_call(
        margins,
        out_shape=[
            shape(8, 128),
            pltpu.VMEM((N, W), BF16),
            shape(1, W),
            shape(NB, OWN, dtype=BF16),
        ],
        in_specs=[pl.BlockSpec(memory_space=pltpu.HBM), VMEM, VMEM, VMEM, SMEM],
        out_specs=[VMEM] * 4,
        scratch_shapes=[pltpu.SemaphoreType.DMA((8,))],
        compiler_params=pltpu.CompilerParams(vmem_limit_bytes=16 << 20),
    )(
        pltpu.with_memory_space_constraint(examples, pltpu.HBM),
        wfloat,
        block_ids.reshape(1, W),
        strengths,
        place,
    )
    margin = margin + swapped(margin)
    margin_parts = lax.all_to_all(
        jnp.broadcast_to(margin[None], (NY * NZ, 8, 128)), ("y", "z"), 0, 0, tiled=True
    )
    part, *sends, curvew = call(
        gradients,
        [shape(R, W), *[shape(R, W + OWN, dtype=BF16)] * (NX - 1), shape(1, N)],
        margin_parts,
        labels.reshape(1, N),
        split.reshape(1, N),
        val_weight,
        examples,
        place,
        smem=(5,),
    )
    wires = [shift(send, "x", NX, s + 1) for s, send in enumerate(sends)]
    pair = [shape(R, HALF + 2 * LANES)] * 2
    rhs, lows, keep, send = call(
        first_tangents,
        [shape(R, OWN), shape(NX, R, OWN, dtype=BF16), *pair],
        part,
        *wires,
        examples,
        lamf,
        wfloat,
        onehot,
        place,
        scratch=[pltpu.VMEM((R, N), F32), pltpu.VMEM((R, NB), F32)],
        smem=(8,),
    )
    arrived = summed(keep, send, place)
    tang_first, weighted, kept_first = call(
        weigh,
        [shape(R, HALF), shape(R, HALF + LANES, dtype=BF16), shape(R, 2 * LANES)],
        arrived,
        curvew,
        place,
        smem=(2,),
    )
    part = call(
        products,
        shape(R, W + LANES, dtype=BF16),
        weighted,
        swapped(weighted),
        kept_first,
        examples,
        place,
        smem=(4,),
    )
    resid, keep, send, kept = call(
        second_tangents,
        [shape(R, OWN), *pair, shape(R, LANES)],
        part,
        *shifted(part, "x", NX),
        rhs,
        lows,
        examples,
        lamf,
        wfloat,
        onehot,
        place,
        scratch=[
            pltpu.VMEM((R, N), F32),
            pltpu.VMEM((R, NB), F32),
            pltpu.VMEM((NX, R, OWN), BF16),
        ],
        smem=(10,),
    )
    arrived = summed(keep, send, place)
    out = call(
        curvature,
        shape(NC * NX, R, LANES),
        arrived,
        curvew,
        tang_first,
        kept_first,
        place,
        smem=(4,),
    )
    arrived = lax.all_to_all(out, ("c", "x"), 0, 0, tiled=True)
    solve, hyper = call(
        finish,
        [shape(R, OWN), shape(1, R)],
        arrived,
        kept,
        rhs,
        resid,
        strengths,
        place,
        smem=(5,),
    )
    return solve, hyper.reshape(R, 1)


def solution(mesh):
    fine = Mesh(mesh.devices.reshape(NY, NZ, NC, NX), ("y", "z", "c", "x"))
    feat = ("y", "z", "c")
    placed = (P("x", feat), P(feat), P("x"), P("x"), P(None, "x"), P(), P(feat))
    return jax.shard_map(
        shards,
        mesh=fine,
        in_specs=placed,
        out_specs=(P(None, (*feat, "x")), P(None, (*feat, "x"))),
        check_vma=False,
    )
```

```python
import jax
import jax.numpy as jnp
from jax import lax
from jax.experimental import pallas as pl
from jax.experimental.pallas import tpu as pltpu
from jax.sharding import Mesh
from jax.sharding import PartitionSpec as P

F32 = jnp.float32
BF16 = jnp.bfloat16
NT = (((1,), (1,)), ((), ()))
NY, NZ, NC, NX = 4, 8, 2, 4
R = 32
N = 1024
HALF = N // NC
W = 4096
OWN = W // NX
NB = 256
TOTAL = float(N * NX)
LANES = 128
PART = OWN // 2
VMEM = pl.BlockSpec(memory_space=pltpu.VMEM)
SMEM = pl.BlockSpec(memory_space=pltpu.SMEM)
HBM = pl.BlockSpec(memory_space=pltpu.HBM)


def call(body, outs, *arrays, scratch=(), limit=16, smem=(), hbm=(), flops=0):
    specs = [SMEM if i in smem else HBM if i in hbm else VMEM for i in range(len(arrays))]
    arrays = [
        pltpu.with_memory_space_constraint(a, pltpu.HBM) if i in hbm else a
        for i, a in enumerate(arrays)
    ]
    return pl.pallas_call(
        body,
        out_shape=outs,
        in_specs=specs,
        out_specs=jax.tree.map(lambda _: VMEM, outs),
        scratch_shapes=scratch,
        compiler_params=pltpu.CompilerParams(vmem_limit_bytes=limit << 20),
        cost_estimate=pl.CostEstimate(flops=flops, bytes_accessed=4 << 20, transcendentals=0),
    )(*arrays)


def shape(*dims, dtype=F32):
    return jax.ShapeDtypeStruct(dims, dtype)


def lane_ids(lanes=LANES):
    return lax.broadcasted_iota(jnp.int32, (R, lanes), 1)


def column(tile, lane):
    return jnp.sum(jnp.where(lane_ids(tile.shape[1]) == lane, tile, 0.0), axis=1, keepdims=True)


def columns(values, first=0):
    lanes = lane_ids()
    tile = jnp.zeros((R, LANES), F32)
    for i, value in enumerate(values):
        tile = jnp.where(lanes == first + i, value, tile)
    return tile


def terms(value, count):
    found = []
    for _ in range(count):
        term = value.astype(BF16).astype(F32)
        found.append(term)
        value = value - term
    return found


def to_terms(tile):
    first, second, third = terms(tile, 3)
    return first + pltpu.roll(second, 8, 1) + pltpu.roll(third, 16, 1)


def from_terms(tile):
    total = tile + pltpu.roll(tile, LANES - 8, 1) + pltpu.roll(tile, LANES - 16, 1)
    return jnp.where(lane_ids() < 8, total, 0.0)


def chunk(index, size):
    return pl.ds(pl.multiple_of(index * size, size), size)


def block_sums(vec, weight, onehot):
    parts = jnp.concatenate(terms(vec * weight, 3), axis=0).astype(BF16)
    sums = lax.dot_general(parts, onehot, NT, preferred_element_type=F32)
    return sums[:R] + sums[R : 2 * R] + sums[2 * R :]


def prepare(ids, strengths, place, gradw, lamf, onehot):
    kinds = lax.broadcasted_iota(jnp.int32, (NB, OWN), 0)
    rows = lax.broadcasted_iota(jnp.int32, (16, NB), 0)
    split3 = jnp.zeros((16, NB), F32)
    for i, term in enumerate(terms(strengths[...], 3)):
        split3 = jnp.where(rows == i, term, split3)
    split3 = split3.astype(BF16)
    for j in range(NX):
        hot = (kinds == ids[:, j * OWN : (j + 1) * OWN]).astype(F32).astype(BF16)
        found = jnp.dot(split3, hot, preferred_element_type=F32)
        lamf[:, j * OWN : (j + 1) * OWN] = found[0:1] + found[1:2] + found[2:3]
    own = ids[:, chunk(place[3], OWN)]
    core = lax.shift_right_logical(own, 2) & 1
    moved = core * 128 + lax.shift_right_logical(own, 3) * 4 + (own & 3)
    onehot[...] = (kinds == moved).astype(F32).astype(BF16)


def margins(source, given, place, margin, examples, wfloat, weights, arrival):
    def fetch(i):
        rows = pl.ds(i * 128, 128)
        return pltpu.make_async_copy(source.at[rows], examples.at[rows], arrival.at[i])

    small = pltpu.make_async_copy(given, weights, arrival.at[8])
    small.start()
    for i in range(3):
        fetch(i).start()
    small.wait()
    lines = weights[...].astype(F32)
    line = jnp.concatenate([lines[i : i + 1] for i in range(W // LANES)], axis=1)
    wfloat[...] = line
    rhs = jnp.broadcast_to(line, (16, W)).astype(BF16)
    for i in range(8):
        fetch(i).wait()
        if i + 3 < 8:
            fetch(i + 3).start()
        rows = lax.dot_general(
            rhs, examples[i * 128 : (i + 1) * 128, :], NT, preferred_element_type=F32
        )
        margin[i : i + 1, :] = rows[0:1]


def part_of(owner, which):
    return pl.ds(pl.multiple_of(owner * OWN + which * PART, PART), PART)


def rhs_parts(which, gradw, examples, place, part, sends):
    for k in range(NX):
        found = jnp.dot(
            gradw, examples[:, part_of(k, which)], preferred_element_type=F32
        )
        cols = slice(k * PART, (k + 1) * PART)
        part[:, cols] = found
        high = found.astype(BF16)
        for send in sends:
            send[:, cols] = high
    for s, send in enumerate(sends):
        found = part[:, chunk((place[3] + s + 1) % NX, PART)]
        send[:, NX * PART :] = (found - found.astype(BF16).astype(F32)).astype(BF16)


def gradients(
    margin_parts, labels, split, val_weight, examples, place,
    part, send1, send2, send3, curvew, gradw,
):
    whole = jnp.sum(margin_parts[...], axis=0)
    margin = jnp.concatenate([whole[i : i + 1] for i in range(8)], axis=1)
    prob = 1.0 / (1.0 + jnp.exp(-margin))
    train = split[...].astype(F32)
    curvew[...] = train * prob * (1.0 - prob)
    err = (1.0 - train) * (prob - labels[...].astype(F32))
    found = (val_weight[...] * err / jnp.sqrt(F32(TOTAL))).astype(BF16)
    gradw[...] = found
    rhs_parts(0, found, examples, place, part, (send1, send2, send3))


def gradients_rest(gradw, examples, place, part, send1, send2, send3):
    rhs_parts(1, gradw[...], examples, place, part, (send1, send2, send3))


def tangents(pieces, which, examples, x, before, tang):
    for i in range(N // 256):
        rows = slice(i * 256, (i + 1) * 256)
        total = None if before is None else before[:, rows]
        for s, piece in enumerate(pieces):
            cols = part_of((x - s + NX) % NX, which)
            term = lax.dot_general(
                piece[...], examples[rows, cols], NT, preferred_element_type=F32
            )
            total = term if total is None else total + term
        tang[:, rows] = total


def halves(tang, scalars, blocks, core, keep, send):
    for out, which in ((keep, core), (send, 1 - core)):
        out[:, :HALF] = tang[:, chunk(which, HALF)]
        out[:, HALF : HALF + LANES] = scalars
        out[:, HALF + LANES :] = blocks[:, chunk(which, LANES)]


def first_part(
    which, part, wires, examples, lamf, wfloat, onehot, place, rhs, lows, before, tang
):
    x = place[3]
    for s in range(NX):
        cols = chunk((x - s + NX) % NX, PART)
        vec = part[:, cols] + sum(w[:, cols].astype(F32) for w in wires)
        if s == 0:
            vec = vec + sum(w[:, NX * PART :].astype(F32) for w in wires)
            rhs[...] = vec
            own = part_of(x, which)
            square = vec * vec
            norm = jnp.sum(square, axis=1, keepdims=True)
            scaled = jnp.sum(lamf[:, own] * square, axis=1, keepdims=True)
            hot = onehot[:, which * PART : (which + 1) * PART]
            blocks = block_sums(vec, wfloat[:, own], hot)
        lows[s] = vec.astype(BF16)
    tangents([lows.at[s] for s in range(NX)], which, examples, x, before, tang)
    return columns([norm, scaled]), blocks


def first_tangents(
    part, wire1, wire2, wire3, examples, lamf, wfloat, onehot, place,
    rhs, lows, tang, sums,
):
    scalars, blocks = first_part(
        0, part, (wire1, wire2, wire3), examples, lamf, wfloat, onehot, place,
        rhs, lows, None, tang,
    )
    sums[:, :LANES] = scalars
    sums[:, LANES:] = blocks


def first_tangents_rest(
    part, wire1, wire2, wire3, examples, lamf, wfloat, onehot, before, sums, place,
    rhs, lows, keep, send, tang, total,
):
    scalars, blocks = first_part(
        1, part, (wire1, wire2, wire3), examples, lamf, wfloat, onehot, place,
        rhs, lows, before, tang,
    )
    total[...] = sums[:, LANES:] + blocks
    halves(tang, sums[:, :LANES] + scalars, total, place[2], keep, send)


def to_wire(keep, arrived, wire):
    total = keep[...] + arrived[...]
    wire[:, :HALF] = total[:, :HALF].astype(BF16)
    wire[:, HALF : HALF + LANES] = to_terms(total[:, HALF : HALF + LANES]).astype(BF16)
    high, rest = terms(total[:, HALF + LANES :], 2)
    wire[:, HALF + LANES : HALF + 2 * LANES] = high.astype(BF16)
    wire[:, HALF + 2 * LANES :] = rest.astype(BF16)


def along_y(wire0, wire1, wire2, wire3, place, out):
    total = wire0[...].astype(F32)
    for wire in (wire1, wire2, wire3):
        total = total + wire[...].astype(F32)
    tang = total[:, :HALF].astype(BF16)
    tile = to_terms(from_terms(total[:, HALF : HALF + LANES]))
    blocks = total[:, HALF + LANES : HALF + 2 * LANES] + total[:, HALF + 2 * LANES :]
    high, rest = terms(blocks, 2)
    lanes = lane_ids()
    at64 = pltpu.roll(high, (64 - 32 * place[0] + LANES) % LANES, 1)
    at96 = pltpu.roll(rest, (96 - 32 * place[0] + LANES) % LANES, 1)
    tile = jnp.where(lanes >= 96, at96, jnp.where(lanes >= 64, at64, tile)).astype(BF16)
    for i in range(NZ):
        out[i, :, :HALF] = tang
        out[i, :, HALF:] = tile


def along_z(arrived):
    tang = arrived[0, :, :HALF].astype(F32)
    tile = arrived[0, :, HALF:].astype(F32)
    for i in range(1, NZ):
        tang = tang + arrived[i, :, :HALF].astype(F32)
        tile = tile + arrived[i, :, HALF:].astype(F32)
    blocks = pltpu.roll(tile, 64, 1) + pltpu.roll(tile, 32, 1)
    return tang, from_terms(tile), jnp.where(lane_ids() < 32, blocks, 0.0)


def weigh(arrived, curvew, place, tang_out, weighted, kept):
    tang, scalars, blocks = along_z(arrived)
    tang_out[...] = tang
    half = curvew[:, chunk(place[2], HALF)]
    product = half * tang
    weighted[:, :HALF] = product.astype(BF16)
    curv = columns([jnp.sum(product * tang, axis=1, keepdims=True)], 2)
    weighted[:, HALF:] = to_terms(curv).astype(BF16)
    kept[:, :LANES] = scalars + curv
    kept[:, LANES:] = blocks


def product_parts(which, weighted, other, examples, place, part):
    core = place[2]
    for k in range(NX):
        cols = part_of(k, which)
        mine = jnp.dot(
            weighted[:, :HALF], examples[chunk(core, HALF), cols], preferred_element_type=F32
        )
        rest = jnp.dot(
            other[:, :HALF], examples[chunk(1 - core, HALF), cols], preferred_element_type=F32
        )
        part[:, k * PART : (k + 1) * PART] = (mine + rest).astype(BF16)


def products(weighted, other, kept, examples, place, part):
    scalars = kept[:, :LANES] + from_terms(other[:, HALF:].astype(F32))
    part[:, NX * PART :] = to_terms(scalars).astype(BF16)
    product_parts(0, weighted, other, examples, place, part)


def products_rest(weighted, other, examples, place, part):
    product_parts(1, weighted, other, examples, place, part)


def second_part(
    which, alpha, parts, rhs, lows, examples, lamf, wfloat, onehot, place,
    resid, pieces, before, tang,
):
    x = place[3]
    for s in range(NX):
        owner = (x - s + NX) % NX
        total = sum(p[:, chunk(owner, PART)].astype(F32) for p in parts)
        direc = rhs[...] if s == 0 else lows[s].astype(F32)
        cols = part_of(owner, which)
        lam = lamf[:, cols]
        left = direc - alpha * (total / F32(TOTAL) + lam * direc)
        pieces[s] = left.astype(BF16)
        if s == 0:
            resid[...] = left
            scalars = columns(
                [
                    jnp.sum(left * left, axis=1, keepdims=True),
                    jnp.sum(lam * left * left, axis=1, keepdims=True),
                    jnp.sum(lam * left * direc, axis=1, keepdims=True),
                ]
            )
            hot = onehot[:, which * PART : (which + 1) * PART]
            blocks = block_sums(left, wfloat[:, cols], hot)
    tangents([pieces.at[s] for s in range(NX)], which, examples, x, before, tang)
    return scalars, blocks


def second_tangents(
    part0, part1, part2, part3, rhs, lows, examples, lamf, wfloat, onehot, place,
    resid, tang, sums, kept, pieces,
):
    parts = (part0, part1, part2, part3)
    tile = from_terms(sum(p[:, NX * PART :].astype(F32) for p in parts))
    norm, scaled, curv = (column(tile, i) for i in range(3))
    alpha = norm / (curv / F32(TOTAL) + scaled)
    kept[...] = jnp.where(lane_ids() == 3, alpha, tile)
    scalars, blocks = second_part(
        0, alpha, parts, rhs, lows, examples, lamf, wfloat, onehot, place,
        resid, pieces, None, tang,
    )
    sums[:, :LANES] = scalars
    sums[:, LANES:] = blocks


def second_tangents_rest(
    part0, part1, part2, part3, rhs, lows, examples, lamf, wfloat, onehot, before, sums, kept,
    place, resid, keep, send, tang, total, pieces,
):
    scalars, blocks = second_part(
        1, column(kept[...], 3), (part0, part1, part2, part3), rhs, lows, examples, lamf,
        wfloat, onehot, place, resid, pieces, before, tang,
    )
    total[...] = sums[:, LANES:] + blocks
    halves(tang, sums[:, :LANES] + scalars, total, place[2], keep, send)


def curvature(arrived, curvew, tang_first, kept, place, out):
    tang, scalars, blocks = along_z(arrived)
    half = curvew[:, chunk(place[2], HALF)]
    product = half * tang
    both = jnp.sum(product * tang, axis=1, keepdims=True)
    cross = jnp.sum(product * tang_first[...], axis=1, keepdims=True)
    tile = jnp.where(lane_ids() < 3, scalars, columns([both, cross], 3))
    lanes = lane_ids()
    shift = 4 * place[1]
    now = pltpu.roll(blocks, (32 - shift + LANES) % LANES, 1)
    before = pltpu.roll(kept[:, LANES:], (36 - shift + LANES) % LANES, 1)
    tile = jnp.where((lanes >= 32) & (lanes < 36), now, tile)
    tile = jnp.where((lanes >= 36) & (lanes < 40), before, tile)
    for i in range(NC * NX):
        out[i] = tile


def finish(
    arrived, kept, rhs_a, rhs_b, resid_a, resid_b, strengths, place, solve, hyper
):
    core, x = place[2], place[3]
    mine = sum(arrived[core * NX + i] for i in range(NX))
    rest = sum(arrived[(1 - core) * NX + i] for i in range(NX))
    every = mine + rest
    tile = kept[...]
    norm, scaled_first, curv_first, alpha = (column(tile, i) for i in range(4))
    norm_next, scaled, mixed = (column(mine, i) for i in range(3))
    both, cross = column(every, 3), column(every, 4)
    beta = norm_next / norm
    curv = (both + 2.0 * beta * cross + beta * beta * curv_first) / F32(TOTAL)
    curv = curv + (scaled + 2.0 * beta * mixed + beta * beta * scaled_first)
    alpha_next = norm_next / curv
    for i, (rhs, resid) in enumerate(((rhs_a, resid_a), (rhs_b, resid_b))):
        first = rhs[...]
        solve[:, i * PART : (i + 1) * PART] = alpha * first + alpha_next * (
            resid[...] + beta * first
        )
    now, before = column(mine, 32 + x), column(mine, 36 + x)
    block = ((place[0] * NZ + place[1]) * NC + core) * NX + x
    kinds = lax.broadcasted_iota(jnp.int32, (1, NB), 1)
    strength = jnp.sum(jnp.where(kinds == block, strengths[...], 0.0), axis=1, keepdims=True)
    found = -strength * (alpha * before + alpha_next * (now + beta * before))
    hyper[...] = jnp.transpose(jnp.broadcast_to(found, (R, LANES)))[0:1]


def shift(array, axis, length, by):
    return lax.ppermute(array, axis, [(i, (i + by) % length) for i in range(length)])


def shifted(array, axis, length):
    return [shift(array, axis, length, s) for s in range(1, length)]


def swapped(array):
    return lax.ppermute(array, "c", [(0, 1), (1, 0)])


def summed(keep, send, place):
    wire = call(to_wire, shape(R, HALF + 3 * LANES, dtype=BF16), keep, swapped(send))
    arrived = shifted(wire, "y", NY)
    out = call(
        along_y, shape(NZ, R, HALF + LANES, dtype=BF16), wire, *arrived, place, smem=(4,)
    )
    return lax.all_to_all(out, "z", 0, 0, tiled=True)


def shards(examples, weights, labels, split, val_weight, strengths, block_ids):
    place = jnp.stack([lax.axis_index(axis) for axis in ("y", "z", "c", "x")]).astype(jnp.int32)
    strengths = strengths.reshape(1, NB)
    margin, examples, wfloat = call(
        margins,
        [shape(8, 128), pltpu.VMEM((N, W), BF16), shape(1, W)],
        examples,
        weights.reshape(W // LANES, LANES),
        place,
        scratch=[pltpu.VMEM((W // LANES, LANES), BF16), pltpu.SemaphoreType.DMA((9,))],
        hbm=(0, 1),
        smem=(2,),
    )
    margin = margin + swapped(margin)
    margin_parts = lax.all_to_all(
        jnp.broadcast_to(margin[None], (NY * NZ, 8, 128)), ("y", "z"), 0, 0, tiled=True
    )
    work = 2 * R * N * W // 2
    sends = [shape(R, (NX + 1) * PART, dtype=BF16)] * (NX - 1)
    part_a, *sends_a, curvew, gradw = call(
        gradients,
        [shape(R, NX * PART), *sends, shape(1, N), shape(R, N, dtype=BF16)],
        margin_parts,
        labels.reshape(1, N),
        split.reshape(1, N),
        val_weight,
        examples,
        place,
        smem=(5,),
        flops=work,
    )
    wires_a = [shift(send, "x", NX, s + 1) for s, send in enumerate(sends_a)]
    part_b, *sends_b = call(
        gradients_rest,
        [shape(R, NX * PART), *sends],
        gradw,
        examples,
        place,
        smem=(2,),
        flops=work,
    )
    lamf, onehot = call(
        prepare,
        [shape(1, W), shape(NB, OWN, dtype=BF16)],
        block_ids.reshape(1, W),
        strengths,
        place,
        gradw,
        smem=(2,),
    )
    wires_b = [shift(send, "x", NX, s + 1) for s, send in enumerate(sends_b)]
    pair = [shape(R, HALF + 2 * LANES)] * 2
    low = shape(NX, R, PART, dtype=BF16)
    rhs_a, lows_a, tang, sums = call(
        first_tangents,
        [shape(R, PART), low, shape(R, N), shape(R, LANES + NB)],
        part_a,
        *wires_a,
        examples,
        lamf,
        wfloat,
        onehot,
        place,
        smem=(8,),
        flops=work,
    )
    rhs_b, lows_b, keep, send = call(
        first_tangents_rest,
        [shape(R, PART), low, *pair],
        part_b,
        *wires_b,
        examples,
        lamf,
        wfloat,
        onehot,
        tang,
        sums,
        place,
        scratch=[pltpu.VMEM((R, N), F32), pltpu.VMEM((R, NB), F32)],
        smem=(10,),
        flops=work,
    )
    arrived = summed(keep, send, place)
    tang_first, weighted, kept_first = call(
        weigh,
        [shape(R, HALF), shape(R, HALF + LANES, dtype=BF16), shape(R, 2 * LANES)],
        arrived,
        curvew,
        place,
        smem=(2,),
    )
    other = swapped(weighted)
    part_a = call(
        products,
        shape(R, NX * PART + LANES, dtype=BF16),
        weighted,
        other,
        kept_first,
        examples,
        place,
        smem=(4,),
        flops=work,
    )
    wires_a = shifted(part_a, "x", NX)
    part_b = call(
        products_rest,
        shape(R, NX * PART, dtype=BF16),
        weighted,
        other,
        examples,
        place,
        smem=(3,),
        flops=work,
    )
    wires_b = shifted(part_b, "x", NX)
    resid_a, tang, sums, kept = call(
        second_tangents,
        [shape(R, PART), shape(R, N), shape(R, LANES + NB), shape(R, LANES)],
        part_a,
        *wires_a,
        rhs_a,
        lows_a,
        examples,
        lamf,
        wfloat,
        onehot,
        place,
        scratch=[pltpu.VMEM((NX, R, PART), BF16)],
        smem=(10,),
        flops=work,
    )
    resid_b, keep, send = call(
        second_tangents_rest,
        [shape(R, PART), *pair],
        part_b,
        *wires_b,
        rhs_b,
        lows_b,
        examples,
        lamf,
        wfloat,
        onehot,
        tang,
        sums,
        kept,
        place,
        scratch=[
            pltpu.VMEM((R, N), F32),
            pltpu.VMEM((R, NB), F32),
            pltpu.VMEM((NX, R, PART), BF16),
        ],
        smem=(13,),
        flops=work,
    )
    arrived = summed(keep, send, place)
    out = call(
        curvature,
        shape(NC * NX, R, LANES),
        arrived,
        curvew,
        tang_first,
        kept_first,
        place,
        smem=(4,),
    )
    arrived = lax.all_to_all(out, ("c", "x"), 0, 0, tiled=True)
    solve, hyper = call(
        finish,
        [shape(R, OWN), shape(1, R)],
        arrived,
        kept,
        rhs_a,
        rhs_b,
        resid_a,
        resid_b,
        strengths,
        place,
        smem=(7,),
    )
    return solve, hyper.reshape(R, 1)


def solution(mesh):
    fine = Mesh(mesh.devices.reshape(NY, NZ, NC, NX), ("y", "z", "c", "x"))
    feat = ("y", "z", "c")
    placed = (P("x", feat), P(feat), P("x"), P("x"), P(None, "x"), P(), P(feat))
    return jax.shard_map(
        shards,
        mesh=fine,
        in_specs=placed,
        out_specs=(P(None, (*feat, "x")), P(None, (*feat, "x"))),
        check_vma=False,
    )
```

```python
import functools

import jax
import jax.numpy as jnp
from jax import lax
from jax.experimental import pallas as pl
from jax.experimental.pallas import tpu as pltpu
from jax.sharding import Mesh
from jax.sharding import PartitionSpec as P

F32 = jnp.float32
BF16 = jnp.bfloat16
NT = (((1,), (1,)), ((), ()))
NY, NZ, NC, NX = 4, 8, 2, 4
R = 32
N = 1024
HALF = N // NC
W = 4096
OWN = W // NX
NB = 256
TOTAL = float(N * NX)
LANES = 128
PART = OWN // 2
VMEM = pl.BlockSpec(memory_space=pltpu.VMEM)
HBM = pl.BlockSpec(memory_space=pltpu.HBM)


def call(body, outs, *arrays, scratch=(), limit=16, hbm=(), flops=0):
    specs = [HBM if i in hbm else VMEM for i in range(len(arrays))]
    arrays = [
        pltpu.with_memory_space_constraint(a, pltpu.HBM) if i in hbm else a
        for i, a in enumerate(arrays)
    ]
    return pl.pallas_call(
        body,
        out_shape=outs,
        in_specs=specs,
        out_specs=jax.tree.map(lambda _: VMEM, outs),
        scratch_shapes=scratch,
        compiler_params=pltpu.CompilerParams(vmem_limit_bytes=limit << 20),
        cost_estimate=pl.CostEstimate(flops=flops, bytes_accessed=4 << 20, transcendentals=0),
    )(*arrays)


def shape(*dims, dtype=F32):
    return jax.ShapeDtypeStruct(dims, dtype)


def lane_ids(lanes=LANES):
    return lax.broadcasted_iota(jnp.int32, (R, lanes), 1)


def column(tile, lane):
    return jnp.sum(jnp.where(lane_ids(tile.shape[1]) == lane, tile, 0.0), axis=1, keepdims=True)


def columns(values, first=0):
    lanes = lane_ids()
    tile = jnp.zeros((R, LANES), F32)
    for i, value in enumerate(values):
        tile = jnp.where(lanes == first + i, value, tile)
    return tile


def terms(value, count):
    found = []
    for _ in range(count):
        term = value.astype(BF16).astype(F32)
        found.append(term)
        value = value - term
    return found


def to_terms(tile):
    first, second, third = terms(tile, 3)
    return first + pltpu.roll(second, 8, 1) + pltpu.roll(third, 16, 1)


def from_terms(tile):
    total = tile + pltpu.roll(tile, LANES - 8, 1) + pltpu.roll(tile, LANES - 16, 1)
    return jnp.where(lane_ids() < 8, total, 0.0)


def chunk(index, size):
    return pl.ds(pl.multiple_of(index * size, size), size)


def block_sums(vec, weight, onehot):
    parts = jnp.concatenate(terms(vec * weight, 3), axis=0).astype(BF16)
    sums = lax.dot_general(parts, onehot, NT, preferred_element_type=F32)
    return sums[:R] + sums[R : 2 * R] + sums[2 * R :]


def prepare(ids, strengths, place, gradw, lamf, onehot):
    kinds = lax.broadcasted_iota(jnp.int32, (NB, OWN), 0)
    rows = lax.broadcasted_iota(jnp.int32, (16, NB), 0)
    split3 = jnp.zeros((16, NB), F32)
    for i, term in enumerate(terms(strengths[...], 3)):
        split3 = jnp.where(rows == i, term, split3)
    split3 = split3.astype(BF16)
    for j in range(NX):
        hot = (kinds == ids[:, j * OWN : (j + 1) * OWN]).astype(F32).astype(BF16)
        found = jnp.dot(split3, hot, preferred_element_type=F32)
        lamf[:, j * OWN : (j + 1) * OWN] = found[0:1] + found[1:2] + found[2:3]
    own = ids[:, chunk(place[0, 3], OWN)]
    core = lax.shift_right_logical(own, 2) & 1
    moved = core * 128 + lax.shift_right_logical(own, 3) * 4 + (own & 3)
    onehot[...] = (kinds == moved).astype(F32).astype(BF16)


def margins(source, given, place, margin, examples, wfloat, weights, arrival):
    width = W // 8

    def fetch(i):
        at = (slice(None), pl.ds(i * width, width))
        return pltpu.make_async_copy(source.at[at], examples.at[at], arrival.at[i])

    small = pltpu.make_async_copy(given, weights, arrival.at[8])
    small.start()
    for i in range(8):
        fetch(i).start()
    small.wait()
    lines = weights[...].astype(F32)
    line = jnp.concatenate([lines[i : i + 1] for i in range(W // LANES)], axis=1)
    wfloat[...] = line
    rhs = jnp.broadcast_to(line, (16, W)).astype(BF16)
    total = None
    for i in range(8):
        fetch(i).wait()
        cols = slice(i * width, (i + 1) * width)
        term = lax.dot_general(
            rhs[:, cols], examples[:, cols], NT, preferred_element_type=F32
        )
        total = term if total is None else total + term
    for i in range(8):
        margin[i : i + 1, :] = total[0:1, i * LANES : (i + 1) * LANES]


def partner(x, which, stage):
    return x ^ (1 if which == stage else 3)


def part_of(owner, which):
    return pl.ds(pl.multiple_of(owner * OWN + which * PART, PART), PART)


def rhs_parts(which, gradw, examples, place, part, wire):
    x = place[0, 3]
    for k in range(NX):
        found = jnp.dot(
            gradw, examples[:, part_of(k, which)], preferred_element_type=F32
        )
        cols = slice(k * PART, (k + 1) * PART)
        part[:, cols] = found
        wire[:, cols] = found.astype(BF16)
    for i, owner in enumerate((partner(x, which, 0), x ^ 2)):
        found = part[:, chunk(owner, PART)]
        rest = found - found.astype(BF16).astype(F32)
        wire[:, (NX + i) * PART : (NX + i + 1) * PART] = rest.astype(BF16)


def gradients(
    margin_parts, labels, split, val_weight, examples, place, part, wire, curvew, gradw
):
    whole = jnp.sum(margin_parts[...], axis=0)
    margin = jnp.concatenate([whole[i : i + 1] for i in range(8)], axis=1)
    prob = 1.0 / (1.0 + jnp.exp(-margin))
    train = split[...].astype(F32)
    curvew[...] = train * prob * (1.0 - prob)
    err = (1.0 - train) * (prob - labels[...].astype(F32))
    found = (val_weight[...] * err / jnp.sqrt(F32(TOTAL))).astype(BF16)
    gradw[...] = found
    rhs_parts(0, found, examples, place, part, wire)


def gradients_rest(gradw, examples, place, part, wire):
    rhs_parts(1, gradw[...], examples, place, part, wire)


def rhs_pairs(which, part, arrived, place, both, wire):
    x = place[0, 3]
    other = partner(x, which, 1)
    both[...] = part[...] + arrived[:, : NX * PART].astype(F32)
    for i, owner in enumerate((x, other)):
        rest = arrived[:, (NX + i) * PART : (NX + i + 1) * PART].astype(F32)
        both[:, chunk(owner, PART)] += rest
    wire[:, : NX * PART] = both[...].astype(BF16)
    found = both[:, chunk(other, PART)]
    wire[:, NX * PART :] = (found - found.astype(BF16).astype(F32)).astype(BF16)


def tangents(pieces, which, examples, before, tang):
    for i in range(N // 256):
        rows = slice(i * 256, (i + 1) * 256)
        total = None if before is None else before[:, rows]
        for k in range(NX):
            term = lax.dot_general(
                pieces[:, k * PART : (k + 1) * PART],
                examples[rows, part_of(k, which)],
                NT,
                preferred_element_type=F32,
            )
            total = term if total is None else total + term
        tang[:, rows] = total


def halves(tang, scalars, blocks, core, keep, send):
    for out, which in ((keep, core), (send, 1 - core)):
        out[:, :HALF] = tang[:, chunk(which, HALF)]
        out[:, HALF : HALF + LANES] = scalars
        out[:, HALF + LANES :] = blocks[:, chunk(which, LANES)]


def first_part(
    which, part, wire, examples, lamf, wfloat, onehot, place, rhs, lows, before, tang
):
    x = place[0, 3]
    lows[...] = (part[...] + wire[:, : NX * PART].astype(F32)).astype(BF16)
    cols = chunk(x, PART)
    vec = part[:, cols] + wire[:, cols].astype(F32) + wire[:, NX * PART :].astype(F32)
    rhs[...] = vec
    lows[:, cols] = vec.astype(BF16)
    own = part_of(x, which)
    square = vec * vec
    norm = jnp.sum(square, axis=1, keepdims=True)
    scaled = jnp.sum(lamf[:, own] * square, axis=1, keepdims=True)
    hot = onehot[:, which * PART : (which + 1) * PART]
    blocks = block_sums(vec, wfloat[:, own], hot)
    tangents(lows, which, examples, before, tang)
    return columns([norm, scaled]), blocks


def first_tangents(
    part, wire, examples, lamf, wfloat, onehot, place, rhs, lows, tang, sums
):
    scalars, blocks = first_part(
        0, part, wire, examples, lamf, wfloat, onehot, place, rhs, lows, None, tang
    )
    sums[:, :LANES] = scalars
    sums[:, LANES:] = blocks


def first_tangents_rest(
    part, wire, examples, lamf, wfloat, onehot, before, sums, place,
    rhs, lows, keep, send, tang, total,
):
    scalars, blocks = first_part(
        1, part, wire, examples, lamf, wfloat, onehot, place, rhs, lows, before, tang
    )
    total[...] = sums[:, LANES:] + blocks
    halves(tang, sums[:, :LANES] + scalars, total, place[0, 2], keep, send)


def to_wire(keep, arrived, wire):
    total = keep[...] + arrived[...]
    wire[:, :HALF] = total[:, :HALF].astype(BF16)
    wire[:, HALF : HALF + LANES] = to_terms(total[:, HALF : HALF + LANES]).astype(BF16)
    high, rest = terms(total[:, HALF + LANES :], 2)
    wire[:, HALF + LANES : HALF + 2 * LANES] = high.astype(BF16)
    wire[:, HALF + 2 * LANES :] = rest.astype(BF16)


def along_y(wire0, wire1, wire2, wire3, place, out):
    total = wire0[...].astype(F32)
    for wire in (wire1, wire2, wire3):
        total = total + wire[...].astype(F32)
    tang = total[:, :HALF].astype(BF16)
    tile = to_terms(from_terms(total[:, HALF : HALF + LANES]))
    blocks = total[:, HALF + LANES : HALF + 2 * LANES] + total[:, HALF + 2 * LANES :]
    high, rest = terms(blocks, 2)
    lanes = lane_ids()
    at64 = pltpu.roll(high, (64 - 32 * place[0, 0] + LANES) % LANES, 1)
    at96 = pltpu.roll(rest, (96 - 32 * place[0, 0] + LANES) % LANES, 1)
    tile = jnp.where(lanes >= 96, at96, jnp.where(lanes >= 64, at64, tile)).astype(BF16)
    for i in range(NZ):
        out[i, :, :HALF] = tang
        out[i, :, HALF:] = tile


def along_z(arrived):
    tang = arrived[0, :, :HALF].astype(F32)
    tile = arrived[0, :, HALF:].astype(F32)
    for i in range(1, NZ):
        tang = tang + arrived[i, :, :HALF].astype(F32)
        tile = tile + arrived[i, :, HALF:].astype(F32)
    blocks = pltpu.roll(tile, 64, 1) + pltpu.roll(tile, 32, 1)
    return tang, from_terms(tile), jnp.where(lane_ids() < 32, blocks, 0.0)


def weigh(arrived, curvew, place, tang_out, weighted, kept):
    tang, scalars, blocks = along_z(arrived)
    tang_out[...] = tang
    half = curvew[:, chunk(place[0, 2], HALF)]
    product = half * tang
    weighted[:, :HALF] = product.astype(BF16)
    curv = columns([jnp.sum(product * tang, axis=1, keepdims=True)], 2)
    weighted[:, HALF:] = to_terms(curv).astype(BF16)
    kept[:, :LANES] = scalars + curv
    kept[:, LANES:] = blocks


def product_parts(which, weighted, other, examples, place, part):
    core = place[0, 2]
    for k in range(NX):
        cols = part_of(k, which)
        mine = jnp.dot(
            weighted[:, :HALF], examples[chunk(core, HALF), cols], preferred_element_type=F32
        )
        rest = jnp.dot(
            other[:, :HALF], examples[chunk(1 - core, HALF), cols], preferred_element_type=F32
        )
        part[:, k * PART : (k + 1) * PART] = (mine + rest).astype(BF16)


def products(weighted, other, kept, examples, place, part):
    scalars = kept[:, :LANES] + from_terms(other[:, HALF:].astype(F32))
    part[:, NX * PART :] = to_terms(scalars).astype(BF16)
    product_parts(0, weighted, other, examples, place, part)


def products_rest(weighted, other, examples, place, part):
    product_parts(1, weighted, other, examples, place, part)


def product_pairs(mine, other, wire):
    both = mine[...].astype(F32) + other[...].astype(F32)
    wire[:, : NX * PART] = both[:, : NX * PART].astype(BF16)
    if mine.shape[1] > NX * PART:
        wire[:, NX * PART :] = to_terms(from_terms(both[:, NX * PART :])).astype(BF16)


def second_part(
    which, alpha, mine, other, rhs, lows, examples, lamf, wfloat, onehot, place,
    resid, pieces, before, tang,
):
    def step(cols, lam, direc):
        total = mine[:, cols].astype(F32) + other[:, cols].astype(F32)
        return direc - alpha * (total / F32(TOTAL) + lam * direc)

    for k in range(NX):
        cols = slice(k * PART, (k + 1) * PART)
        left = step(cols, lamf[:, part_of(k, which)], lows[:, cols].astype(F32))
        pieces[:, cols] = left.astype(BF16)
    x = place[0, 3]
    own = part_of(x, which)
    cols = chunk(x, PART)
    lam = lamf[:, own]
    direc = rhs[...]
    left = step(cols, lam, direc)
    resid[...] = left
    pieces[:, cols] = left.astype(BF16)
    scalars = columns(
        [
            jnp.sum(left * left, axis=1, keepdims=True),
            jnp.sum(lam * left * left, axis=1, keepdims=True),
            jnp.sum(lam * left * direc, axis=1, keepdims=True),
        ]
    )
    hot = onehot[:, which * PART : (which + 1) * PART]
    blocks = block_sums(left, wfloat[:, own], hot)
    tangents(pieces, which, examples, before, tang)
    return scalars, blocks


def second_tangents(
    mine, other, rhs, lows, examples, lamf, wfloat, onehot, place,
    resid, tang, sums, kept, pieces,
):
    tile = mine[:, NX * PART :].astype(F32) + other[:, NX * PART :].astype(F32)
    tile = from_terms(tile)
    norm, scaled, curv = (column(tile, i) for i in range(3))
    alpha = norm / (curv / F32(TOTAL) + scaled)
    kept[...] = jnp.where(lane_ids() == 3, alpha, tile)
    scalars, blocks = second_part(
        0, alpha, mine, other, rhs, lows, examples, lamf, wfloat, onehot, place,
        resid, pieces, None, tang,
    )
    sums[:, :LANES] = scalars
    sums[:, LANES:] = blocks


def second_tangents_rest(
    mine, other, rhs, lows, examples, lamf, wfloat, onehot, before, sums, kept,
    place, resid, keep, send, tang, total, pieces,
):
    scalars, blocks = second_part(
        1, column(kept[...], 3), mine, other, rhs, lows, examples, lamf,
        wfloat, onehot, place, resid, pieces, before, tang,
    )
    total[...] = sums[:, LANES:] + blocks
    halves(tang, sums[:, :LANES] + scalars, total, place[0, 2], keep, send)


def curvature(arrived, curvew, tang_first, kept, place, out):
    tang, scalars, blocks = along_z(arrived)
    half = curvew[:, chunk(place[0, 2], HALF)]
    product = half * tang
    both = jnp.sum(product * tang, axis=1, keepdims=True)
    cross = jnp.sum(product * tang_first[...], axis=1, keepdims=True)
    tile = jnp.where(lane_ids() < 3, scalars, columns([both, cross], 3))
    lanes = lane_ids()
    shift = 4 * place[0, 1]
    now = pltpu.roll(blocks, (32 - shift + LANES) % LANES, 1)
    before = pltpu.roll(kept[:, LANES:], (36 - shift + LANES) % LANES, 1)
    tile = jnp.where((lanes >= 32) & (lanes < 36), now, tile)
    tile = jnp.where((lanes >= 36) & (lanes < 40), before, tile)
    for i in range(NC * NX):
        out[i] = tile


def finish(
    arrived, kept, rhs_a, rhs_b, resid_a, resid_b, strengths, place, solve, hyper
):
    core, x = place[0, 2], place[0, 3]
    mine = sum(arrived[core * NX + i] for i in range(NX))
    rest = sum(arrived[(1 - core) * NX + i] for i in range(NX))
    every = mine + rest
    tile = kept[...]
    norm, scaled_first, curv_first, alpha = (column(tile, i) for i in range(4))
    norm_next, scaled, mixed = (column(mine, i) for i in range(3))
    both, cross = column(every, 3), column(every, 4)
    beta = norm_next / norm
    curv = (both + 2.0 * beta * cross + beta * beta * curv_first) / F32(TOTAL)
    curv = curv + (scaled + 2.0 * beta * mixed + beta * beta * scaled_first)
    alpha_next = norm_next / curv
    for i, (rhs, resid) in enumerate(((rhs_a, resid_a), (rhs_b, resid_b))):
        first = rhs[...]
        solve[:, i * PART : (i + 1) * PART] = alpha * first + alpha_next * (
            resid[...] + beta * first
        )
    now, before = column(mine, 32 + x), column(mine, 36 + x)
    block = ((place[0, 0] * NZ + place[0, 1]) * NC + core) * NX + x
    kinds = lax.broadcasted_iota(jnp.int32, (1, NB), 1)
    strength = jnp.sum(jnp.where(kinds == block, strengths[...], 0.0), axis=1, keepdims=True)
    found = -strength * (alpha * before + alpha_next * (now + beta * before))
    hyper[...] = jnp.transpose(jnp.broadcast_to(found, (R, LANES)))[0:1]


def shift(array, axis, length, by):
    return lax.ppermute(array, axis, [(i, (i + by) % length) for i in range(length)])


def shifted(array, axis, length):
    return [shift(array, axis, length, s) for s in range(1, length)]


def traded(array, which, stage):
    return lax.ppermute(array, "x", [(i, partner(i, which, stage)) for i in range(NX)])


def swapped(array):
    return lax.ppermute(array, "c", [(0, 1), (1, 0)])


def summed(keep, send, place):
    wire = call(to_wire, shape(R, HALF + 3 * LANES, dtype=BF16), keep, swapped(send))
    arrived = shifted(wire, "y", NY)
    out = call(
        along_y, shape(NZ, R, HALF + LANES, dtype=BF16), wire, *arrived, place
    )
    return lax.all_to_all(out, "z", 0, 0, tiled=True)


def shards(examples, weights, labels, split, val_weight, strengths, block_ids):
    place = jnp.stack([lax.axis_index(axis) for axis in ("y", "z", "c", "x")])
    place = place.astype(jnp.int32).reshape(1, 4)
    strengths = strengths.reshape(1, NB)
    margin, examples, wfloat = call(
        margins,
        [shape(8, 128), pltpu.VMEM((N, W), BF16), shape(1, W)],
        examples,
        weights.reshape(W // LANES, LANES),
        place,
        scratch=[pltpu.VMEM((W // LANES, LANES), BF16), pltpu.SemaphoreType.DMA((9,))],
        hbm=(0, 1),
    )
    margin = margin + swapped(margin)
    margin_parts = lax.all_to_all(
        jnp.broadcast_to(margin[None], (NY * NZ, 8, 128)), ("y", "z"), 0, 0, tiled=True
    )
    work = 2 * R * N * W // 2
    whole = shape(R, NX * PART)
    part_a, wire_a, curvew, gradw = call(
        gradients,
        [
            whole,
            shape(R, (NX + 2) * PART, dtype=BF16),
            shape(1, N),
            shape(R, N, dtype=BF16),
        ],
        margin_parts,
        labels.reshape(1, N),
        split.reshape(1, N),
        val_weight,
        examples,
        place,
        flops=work,
    )
    arrived_a = traded(wire_a, 0, 0)
    part_b, wire_b = call(
        gradients_rest,
        [whole, shape(R, (NX + 2) * PART, dtype=BF16)],
        gradw,
        examples,
        place,
        flops=work,
    )
    arrived_b = traded(wire_b, 1, 0)
    lamf, onehot = call(
        prepare,
        [shape(1, W), shape(NB, OWN, dtype=BF16)],
        block_ids.reshape(1, W),
        strengths,
        place,
        gradw,
    )
    part_a, wire_a = call(
        functools.partial(rhs_pairs, 0),
        [whole, shape(R, (NX + 1) * PART, dtype=BF16)],
        part_a,
        arrived_a,
        place,
    )
    wire_a = traded(wire_a, 0, 1)
    part_b, wire_b = call(
        functools.partial(rhs_pairs, 1),
        [whole, shape(R, (NX + 1) * PART, dtype=BF16)],
        part_b,
        arrived_b,
        place,
    )
    wire_b = traded(wire_b, 1, 1)
    pair = [shape(R, HALF + 2 * LANES)] * 2
    low = shape(R, NX * PART, dtype=BF16)
    rhs_a, lows_a, tang, sums = call(
        first_tangents,
        [shape(R, PART), low, shape(R, N), shape(R, LANES + NB)],
        part_a,
        wire_a,
        examples,
        lamf,
        wfloat,
        onehot,
        place,
        flops=work,
    )
    rhs_b, lows_b, keep, send = call(
        first_tangents_rest,
        [shape(R, PART), low, *pair],
        part_b,
        wire_b,
        examples,
        lamf,
        wfloat,
        onehot,
        tang,
        sums,
        place,
        scratch=[pltpu.VMEM((R, N), F32), pltpu.VMEM((R, NB), F32)],
        flops=work,
    )
    arrived = summed(keep, send, place)
    tang_first, weighted, kept_first = call(
        weigh,
        [shape(R, HALF), shape(R, HALF + LANES, dtype=BF16), shape(R, 2 * LANES)],
        arrived,
        curvew,
        place,
    )
    other = swapped(weighted)
    part_a = call(
        products,
        shape(R, NX * PART + LANES, dtype=BF16),
        weighted,
        other,
        kept_first,
        examples,
        place,
        flops=work,
    )
    arrived_a = traded(part_a, 0, 0)
    part_b = call(
        products_rest,
        shape(R, NX * PART, dtype=BF16),
        weighted,
        other,
        examples,
        place,
        flops=work,
    )
    arrived_b = traded(part_b, 1, 0)
    mine_a = call(
        product_pairs, shape(R, NX * PART + LANES, dtype=BF16), part_a, arrived_a
    )
    other_a = traded(mine_a, 0, 1)
    mine_b = call(product_pairs, shape(R, NX * PART, dtype=BF16), part_b, arrived_b)
    other_b = traded(mine_b, 1, 1)
    resid_a, tang, sums, kept = call(
        second_tangents,
        [shape(R, PART), shape(R, N), shape(R, LANES + NB), shape(R, LANES)],
        mine_a,
        other_a,
        rhs_a,
        lows_a,
        examples,
        lamf,
        wfloat,
        onehot,
        place,
        scratch=[pltpu.VMEM((R, NX * PART), BF16)],
        flops=work,
    )
    resid_b, keep, send = call(
        second_tangents_rest,
        [shape(R, PART), *pair],
        mine_b,
        other_b,
        rhs_b,
        lows_b,
        examples,
        lamf,
        wfloat,
        onehot,
        tang,
        sums,
        kept,
        place,
        scratch=[
            pltpu.VMEM((R, N), F32),
            pltpu.VMEM((R, NB), F32),
            pltpu.VMEM((R, NX * PART), BF16),
        ],
        flops=work,
    )
    arrived = summed(keep, send, place)
    out = call(
        curvature,
        shape(NC * NX, R, LANES),
        arrived,
        curvew,
        tang_first,
        kept_first,
        place,
    )
    arrived = lax.all_to_all(out, ("c", "x"), 0, 0, tiled=True)
    solve, hyper = call(
        finish,
        [shape(R, OWN), shape(1, R)],
        arrived,
        kept,
        rhs_a,
        rhs_b,
        resid_a,
        resid_b,
        strengths,
        place,
    )
    return solve, hyper.reshape(R, 1)


def solution(mesh):
    fine = Mesh(mesh.devices.reshape(NY, NZ, NC, NX), ("y", "z", "c", "x"))
    feat = ("y", "z", "c")
    placed = (P("x", feat), P(feat), P("x"), P("x"), P(None, "x"), P(), P(feat))
    return jax.shard_map(
        shards,
        mesh=fine,
        in_specs=placed,
        out_specs=(P(None, (*feat, "x")), P(None, (*feat, "x"))),
        check_vma=False,
    )
```

```python
import functools

import jax
import jax.numpy as jnp
from jax import lax
from jax.experimental import pallas as pl
from jax.experimental.pallas import tpu as pltpu
from jax.sharding import Mesh
from jax.sharding import PartitionSpec as P

F32 = jnp.float32
BF16 = jnp.bfloat16
NT = (((1,), (1,)), ((), ()))
NY, NZ, NC, NX = 4, 8, 2, 4
R = 32
N = 1024
HALF = N // NC
W = 4096
OWN = W // NX
NB = 256
TOTAL = float(N * NX)
LANES = 128
PART = OWN // 2
VMEM = pl.BlockSpec(memory_space=pltpu.VMEM)
HBM = pl.BlockSpec(memory_space=pltpu.HBM)


def call(body, outs, *arrays, scratch=(), limit=16, hbm=(), flops=0):
    specs = [HBM if i in hbm else VMEM for i in range(len(arrays))]
    arrays = [
        pltpu.with_memory_space_constraint(a, pltpu.HBM) if i in hbm else a
        for i, a in enumerate(arrays)
    ]
    return pl.pallas_call(
        body,
        out_shape=outs,
        in_specs=specs,
        out_specs=jax.tree.map(lambda _: VMEM, outs),
        scratch_shapes=scratch,
        compiler_params=pltpu.CompilerParams(vmem_limit_bytes=limit << 20),
        cost_estimate=pl.CostEstimate(flops=flops, bytes_accessed=4 << 20, transcendentals=0),
    )(*arrays)


def shape(*dims, dtype=F32):
    return jax.ShapeDtypeStruct(dims, dtype)


def lane_ids(lanes=LANES):
    return lax.broadcasted_iota(jnp.int32, (R, lanes), 1)


def column(tile, lane):
    return jnp.sum(jnp.where(lane_ids(tile.shape[1]) == lane, tile, 0.0), axis=1, keepdims=True)


def columns(values, first=0):
    lanes = lane_ids()
    tile = jnp.zeros((R, LANES), F32)
    for i, value in enumerate(values):
        tile = jnp.where(lanes == first + i, value, tile)
    return tile


def terms(value, count):
    found = []
    for _ in range(count):
        term = value.astype(BF16).astype(F32)
        found.append(term)
        value = value - term
    return found


def to_terms(tile):
    first, second, third = terms(tile, 3)
    return first + pltpu.roll(second, 8, 1) + pltpu.roll(third, 16, 1)


def from_terms(tile):
    total = tile + pltpu.roll(tile, LANES - 8, 1) + pltpu.roll(tile, LANES - 16, 1)
    return jnp.where(lane_ids() < 8, total, 0.0)


def chunk(index, size):
    return pl.ds(pl.multiple_of(index * size, size), size)


def block_sums(vec, weight, onehot):
    parts = jnp.concatenate(terms(vec * weight, 3), axis=0).astype(BF16)
    sums = lax.dot_general(parts, onehot, NT, preferred_element_type=F32)
    return sums[:R] + sums[R : 2 * R] + sums[2 * R :]


def prepare(ids, strengths, place, gradw, lamf, onehot):
    kinds = lax.broadcasted_iota(jnp.int32, (NB, OWN), 0)
    rows = lax.broadcasted_iota(jnp.int32, (16, NB), 0)
    split3 = jnp.zeros((16, NB), F32)
    for i, term in enumerate(terms(strengths[...], 3)):
        split3 = jnp.where(rows == i, term, split3)
    split3 = split3.astype(BF16)
    for j in range(NX):
        hot = (kinds == ids[:, j * OWN : (j + 1) * OWN]).astype(F32).astype(BF16)
        found = jnp.dot(split3, hot, preferred_element_type=F32)
        lamf[:, j * OWN : (j + 1) * OWN] = found[0:1] + found[1:2] + found[2:3]
    own = ids[:, chunk(place[0, 3], OWN)]
    core = lax.shift_right_logical(own, 2) & 1
    moved = core * 128 + lax.shift_right_logical(own, 3) * 4 + (own & 3)
    onehot[...] = (kinds == moved).astype(F32).astype(BF16)


def margins(source, given, place, margin, examples, wfloat, weights, arrival):
    width = W // 8

    def fetch(i):
        at = (slice(None), pl.ds(i * width, width))
        return pltpu.make_async_copy(source.at[at], examples.at[at], arrival.at[i])

    small = pltpu.make_async_copy(given, weights, arrival.at[8])
    small.start()
    for i in range(8):
        fetch(i).start()
    small.wait()
    lines = weights[...].astype(F32)
    line = jnp.concatenate([lines[i : i + 1] for i in range(W // LANES)], axis=1)
    wfloat[...] = line
    rhs = jnp.broadcast_to(line, (16, W)).astype(BF16)
    total = None
    for i in range(8):
        fetch(i).wait()
        cols = slice(i * width, (i + 1) * width)
        term = lax.dot_general(
            rhs[:, cols], examples[:, cols], NT, preferred_element_type=F32
        )
        total = term if total is None else total + term
    for i in range(8):
        margin[i : i + 1, :] = total[0:1, i * LANES : (i + 1) * LANES]


def partner(x, which, stage):
    return x ^ (1 if which == stage else 3)


def part_of(owner, which):
    return pl.ds(pl.multiple_of(owner * OWN + which * PART, PART), PART)


def rhs_parts(which, gradw, examples, place, part, wire):
    x = place[0, 3]
    for k in range(NX):
        found = jnp.dot(
            gradw, examples[:, part_of(k, which)], preferred_element_type=F32
        )
        cols = slice(k * PART, (k + 1) * PART)
        part[:, cols] = found
        wire[:, cols] = found.astype(BF16)
    for i, owner in enumerate((partner(x, which, 0), x ^ 2)):
        found = part[:, chunk(owner, PART)]
        rest = found - found.astype(BF16).astype(F32)
        wire[:, (NX + i) * PART : (NX + i + 1) * PART] = rest.astype(BF16)


def gradients(
    margin_parts, labels, split, val_weight, examples, place, part, wire, curvew, gradw
):
    whole = jnp.sum(margin_parts[...], axis=0)
    margin = jnp.concatenate([whole[i : i + 1] for i in range(8)], axis=1)
    prob = 1.0 / (1.0 + jnp.exp(-margin))
    train = split[...].astype(F32)
    curvew[...] = train * prob * (1.0 - prob)
    err = (1.0 - train) * (prob - labels[...].astype(F32))
    found = (val_weight[...] * err / jnp.sqrt(F32(TOTAL))).astype(BF16)
    gradw[...] = found
    rhs_parts(0, found, examples, place, part, wire)


def gradients_rest(gradw, examples, place, part, wire):
    rhs_parts(1, gradw[...], examples, place, part, wire)


def rhs_pairs(which, part, arrived, place, both, wire):
    x = place[0, 3]
    other = partner(x, which, 1)
    both[...] = part[...] + arrived[:, : NX * PART].astype(F32)
    for i, owner in enumerate((x, other)):
        rest = arrived[:, (NX + i) * PART : (NX + i + 1) * PART].astype(F32)
        both[:, chunk(owner, PART)] += rest
    wire[:, : NX * PART] = both[...].astype(BF16)
    found = both[:, chunk(other, PART)]
    wire[:, NX * PART :] = (found - found.astype(BF16).astype(F32)).astype(BF16)


def tangents(pieces, which, examples, before, tang, start, count):
    for i in range(count // 256):
        rows = pl.ds(pl.multiple_of(start + i * 256, 256), 256)
        total = None if before is None else before[:, rows]
        for k in range(NX):
            term = lax.dot_general(
                pieces[:, k * PART : (k + 1) * PART],
                examples[rows, part_of(k, which)],
                NT,
                preferred_element_type=F32,
            )
            total = term if total is None else total + term
        tang[:, i * 256 : (i + 1) * 256] = total


def other_half(pieces, examples, before, scalars, blocks, total, place, send, rest):
    core = place[0, 2]
    tangents(pieces, 1, examples, before, send, (1 - core) * HALF, HALF)
    total[...] = blocks
    send[:, HALF : HALF + LANES] = scalars
    send[:, HALF + LANES :] = total[:, chunk(1 - core, LANES)]
    rest[:, :LANES] = scalars
    rest[:, LANES:] = total[:, chunk(core, LANES)]


def own_half(pieces, examples, before, place, keep):
    tangents(pieces, 1, examples, before, keep, place[0, 2] * HALF, HALF)


def first_part(which, part, wire, lamf, wfloat, onehot, place, rhs, lows):
    x = place[0, 3]
    lows[...] = (part[...] + wire[:, : NX * PART].astype(F32)).astype(BF16)
    cols = chunk(x, PART)
    vec = part[:, cols] + wire[:, cols].astype(F32) + wire[:, NX * PART :].astype(F32)
    rhs[...] = vec
    lows[:, cols] = vec.astype(BF16)
    own = part_of(x, which)
    square = vec * vec
    norm = jnp.sum(square, axis=1, keepdims=True)
    scaled = jnp.sum(lamf[:, own] * square, axis=1, keepdims=True)
    hot = onehot[:, which * PART : (which + 1) * PART]
    blocks = block_sums(vec, wfloat[:, own], hot)
    return columns([norm, scaled]), blocks


def first_tangents(
    part, wire, examples, lamf, wfloat, onehot, place, rhs, lows, tang, sums
):
    scalars, blocks = first_part(0, part, wire, lamf, wfloat, onehot, place, rhs, lows)
    tangents(lows, 0, examples, None, tang, 0, N)
    sums[:, :LANES] = scalars
    sums[:, LANES:] = blocks


def first_tangents_rest(
    part, wire, examples, lamf, wfloat, onehot, before, sums, place,
    rhs, lows, send, rest, total,
):
    scalars, blocks = first_part(1, part, wire, lamf, wfloat, onehot, place, rhs, lows)
    scalars = sums[:, :LANES] + scalars
    blocks = sums[:, LANES:] + blocks
    other_half(lows, examples, before, scalars, blocks, total, place, send, rest)


def to_wire(keep, rest, arrived, wire):
    wire[:, :HALF] = (keep[...] + arrived[:, :HALF]).astype(BF16)
    scalars = rest[:, :LANES] + arrived[:, HALF : HALF + LANES]
    wire[:, HALF : HALF + LANES] = to_terms(scalars).astype(BF16)
    high, low = terms(rest[:, LANES:] + arrived[:, HALF + LANES :], 2)
    wire[:, HALF + LANES : HALF + 2 * LANES] = high.astype(BF16)
    wire[:, HALF + 2 * LANES :] = low.astype(BF16)


def along_y(wire0, wire1, wire2, wire3, place, out):
    total = wire0[...].astype(F32)
    for wire in (wire1, wire2, wire3):
        total = total + wire[...].astype(F32)
    tang = total[:, :HALF].astype(BF16)
    tile = to_terms(from_terms(total[:, HALF : HALF + LANES]))
    blocks = total[:, HALF + LANES : HALF + 2 * LANES] + total[:, HALF + 2 * LANES :]
    high, rest = terms(blocks, 2)
    lanes = lane_ids()
    at64 = pltpu.roll(high, (64 - 32 * place[0, 0] + LANES) % LANES, 1)
    at96 = pltpu.roll(rest, (96 - 32 * place[0, 0] + LANES) % LANES, 1)
    tile = jnp.where(lanes >= 96, at96, jnp.where(lanes >= 64, at64, tile)).astype(BF16)
    for i in range(NZ):
        out[i, :, :HALF] = tang
        out[i, :, HALF:] = tile


def along_z(arrived):
    tang = arrived[0, :, :HALF].astype(F32)
    tile = arrived[0, :, HALF:].astype(F32)
    for i in range(1, NZ):
        tang = tang + arrived[i, :, :HALF].astype(F32)
        tile = tile + arrived[i, :, HALF:].astype(F32)
    blocks = pltpu.roll(tile, 64, 1) + pltpu.roll(tile, 32, 1)
    return tang, from_terms(tile), jnp.where(lane_ids() < 32, blocks, 0.0)


def weigh(arrived, curvew, place, tang_out, weighted, kept):
    tang, scalars, blocks = along_z(arrived)
    tang_out[...] = tang
    half = curvew[:, chunk(place[0, 2], HALF)]
    product = half * tang
    weighted[:, :HALF] = product.astype(BF16)
    curv = columns([jnp.sum(product * tang, axis=1, keepdims=True)], 2)
    weighted[:, HALF:] = to_terms(curv).astype(BF16)
    kept[:, :LANES] = scalars + curv
    kept[:, LANES:] = blocks


def own_products(weighted, examples, place, part_a, part_b):
    rows = chunk(place[0, 2], HALF)
    for which, part in enumerate((part_a, part_b)):
        for k in range(NX):
            part[:, k * PART : (k + 1) * PART] = jnp.dot(
                weighted[:, :HALF],
                examples[rows, part_of(k, which)],
                preferred_element_type=F32,
            )


def product_parts(which, mine, other, examples, place, part):
    rows = chunk(1 - place[0, 2], HALF)
    for k in range(NX):
        cols = slice(k * PART, (k + 1) * PART)
        rest = jnp.dot(
            other[:, :HALF], examples[rows, part_of(k, which)], preferred_element_type=F32
        )
        part[:, cols] = (mine[:, cols] + rest).astype(BF16)


def products(mine, other, kept, examples, place, part):
    scalars = kept[:, :LANES] + from_terms(other[:, HALF:].astype(F32))
    part[:, NX * PART :] = to_terms(scalars).astype(BF16)
    product_parts(0, mine, other, examples, place, part)


def products_rest(mine, other, examples, place, part):
    product_parts(1, mine, other, examples, place, part)


def product_pairs(mine, other, wire):
    both = mine[...].astype(F32) + other[...].astype(F32)
    wire[:, : NX * PART] = both[:, : NX * PART].astype(BF16)
    if mine.shape[1] > NX * PART:
        wire[:, NX * PART :] = to_terms(from_terms(both[:, NX * PART :])).astype(BF16)


def second_part(
    which, alpha, mine, other, rhs, lows, lamf, wfloat, onehot, place, resid, pieces
):
    def step(cols, lam, direc):
        total = mine[:, cols].astype(F32) + other[:, cols].astype(F32)
        return direc - alpha * (total / F32(TOTAL) + lam * direc)

    for k in range(NX):
        cols = slice(k * PART, (k + 1) * PART)
        left = step(cols, lamf[:, part_of(k, which)], lows[:, cols].astype(F32))
        pieces[:, cols] = left.astype(BF16)
    x = place[0, 3]
    own = part_of(x, which)
    cols = chunk(x, PART)
    lam = lamf[:, own]
    direc = rhs[...]
    left = step(cols, lam, direc)
    resid[...] = left
    pieces[:, cols] = left.astype(BF16)
    scalars = columns(
        [
            jnp.sum(left * left, axis=1, keepdims=True),
            jnp.sum(lam * left * left, axis=1, keepdims=True),
            jnp.sum(lam * left * direc, axis=1, keepdims=True),
        ]
    )
    hot = onehot[:, which * PART : (which + 1) * PART]
    blocks = block_sums(left, wfloat[:, own], hot)
    return scalars, blocks


def second_tangents(
    mine, other, rhs, lows, examples, lamf, wfloat, onehot, place,
    resid, tang, sums, kept, pieces,
):
    tile = mine[:, NX * PART :].astype(F32) + other[:, NX * PART :].astype(F32)
    tile = from_terms(tile)
    norm, scaled, curv = (column(tile, i) for i in range(3))
    alpha = norm / (curv / F32(TOTAL) + scaled)
    kept[...] = jnp.where(lane_ids() == 3, alpha, tile)
    scalars, blocks = second_part(
        0, alpha, mine, other, rhs, lows, lamf, wfloat, onehot, place, resid, pieces
    )
    tangents(pieces, 0, examples, None, tang, 0, N)
    sums[:, :LANES] = scalars
    sums[:, LANES:] = blocks


def second_tangents_rest(
    mine, other, rhs, lows, examples, lamf, wfloat, onehot, before, sums, kept,
    place, resid, pieces, send, rest, total,
):
    scalars, blocks = second_part(
        1, column(kept[...], 3), mine, other, rhs, lows, lamf, wfloat, onehot, place,
        resid, pieces,
    )
    scalars = sums[:, :LANES] + scalars
    blocks = sums[:, LANES:] + blocks
    other_half(pieces, examples, before, scalars, blocks, total, place, send, rest)


def curvature(arrived, curvew, tang_first, kept, place, out):
    tang, scalars, blocks = along_z(arrived)
    half = curvew[:, chunk(place[0, 2], HALF)]
    product = half * tang
    both = jnp.sum(product * tang, axis=1, keepdims=True)
    cross = jnp.sum(product * tang_first[...], axis=1, keepdims=True)
    tile = jnp.where(lane_ids() < 3, scalars, columns([both, cross], 3))
    lanes = lane_ids()
    shift = 4 * place[0, 1]
    now = pltpu.roll(blocks, (32 - shift + LANES) % LANES, 1)
    before = pltpu.roll(kept[:, LANES:], (36 - shift + LANES) % LANES, 1)
    tile = jnp.where((lanes >= 32) & (lanes < 36), now, tile)
    tile = jnp.where((lanes >= 36) & (lanes < 40), before, tile)
    for i in range(NC * NX):
        out[i] = tile


def finish(
    arrived, kept, rhs_a, rhs_b, resid_a, resid_b, strengths, place, solve, hyper
):
    core, x = place[0, 2], place[0, 3]
    mine = sum(arrived[core * NX + i] for i in range(NX))
    rest = sum(arrived[(1 - core) * NX + i] for i in range(NX))
    every = mine + rest
    tile = kept[...]
    norm, scaled_first, curv_first, alpha = (column(tile, i) for i in range(4))
    norm_next, scaled, mixed = (column(mine, i) for i in range(3))
    both, cross = column(every, 3), column(every, 4)
    beta = norm_next / norm
    curv = (both + 2.0 * beta * cross + beta * beta * curv_first) / F32(TOTAL)
    curv = curv + (scaled + 2.0 * beta * mixed + beta * beta * scaled_first)
    alpha_next = norm_next / curv
    for i, (rhs, resid) in enumerate(((rhs_a, resid_a), (rhs_b, resid_b))):
        first = rhs[...]
        solve[:, i * PART : (i + 1) * PART] = alpha * first + alpha_next * (
            resid[...] + beta * first
        )
    now, before = column(mine, 32 + x), column(mine, 36 + x)
    block = ((place[0, 0] * NZ + place[0, 1]) * NC + core) * NX + x
    kinds = lax.broadcasted_iota(jnp.int32, (1, NB), 1)
    strength = jnp.sum(jnp.where(kinds == block, strengths[...], 0.0), axis=1, keepdims=True)
    found = -strength * (alpha * before + alpha_next * (now + beta * before))
    hyper[...] = jnp.transpose(jnp.broadcast_to(found, (R, LANES)))[0:1]


def shift(array, axis, length, by):
    return lax.ppermute(array, axis, [(i, (i + by) % length) for i in range(length)])


def traded(array, which, stage):
    return lax.ppermute(array, "x", [(i, partner(i, which, stage)) for i in range(NX)])


def swapped(array):
    return lax.ppermute(array, "c", [(0, 1), (1, 0)])


def summed(pieces, examples, before, send, rest, place, flops):
    arrived = swapped(send)
    keep = call(own_half, shape(R, HALF), pieces, examples, before, place, flops=flops)
    wire = call(to_wire, shape(R, HALF + 3 * LANES, dtype=BF16), keep, rest, arrived)
    far = shift(wire, "y", NY, 2)
    near = [shift(wire, "y", NY, by) for by in (1, NY - 1)]
    out = call(
        along_y, shape(NZ, R, HALF + LANES, dtype=BF16), wire, *near, far, place
    )
    return lax.all_to_all(out, "z", 0, 0, tiled=True)


def shards(examples, weights, labels, split, val_weight, strengths, block_ids):
    place = jnp.stack([lax.axis_index(axis) for axis in ("y", "z", "c", "x")])
    place = place.astype(jnp.int32).reshape(1, 4)
    strengths = strengths.reshape(1, NB)
    margin, examples, wfloat = call(
        margins,
        [shape(8, 128), pltpu.VMEM((N, W), BF16), shape(1, W)],
        examples,
        weights.reshape(W // LANES, LANES),
        place,
        scratch=[pltpu.VMEM((W // LANES, LANES), BF16), pltpu.SemaphoreType.DMA((9,))],
        hbm=(0, 1),
    )
    margin = margin + swapped(margin)
    margin_parts = lax.all_to_all(
        jnp.broadcast_to(margin[None], (NY * NZ, 8, 128)), ("y", "z"), 0, 0, tiled=True
    )
    work = 2 * R * N * W // 2
    whole = shape(R, NX * PART)
    part_a, wire_a, curvew, gradw = call(
        gradients,
        [
            whole,
            shape(R, (NX + 2) * PART, dtype=BF16),
            shape(1, N),
            shape(R, N, dtype=BF16),
        ],
        margin_parts,
        labels.reshape(1, N),
        split.reshape(1, N),
        val_weight,
        examples,
        place,
        flops=work,
    )
    arrived_a = traded(wire_a, 0, 0)
    part_b, wire_b = call(
        gradients_rest,
        [whole, shape(R, (NX + 2) * PART, dtype=BF16)],
        gradw,
        examples,
        place,
        flops=work,
    )
    arrived_b = traded(wire_b, 1, 0)
    lamf, onehot = call(
        prepare,
        [shape(1, W), shape(NB, OWN, dtype=BF16)],
        block_ids.reshape(1, W),
        strengths,
        place,
        gradw,
    )
    part_a, wire_a = call(
        functools.partial(rhs_pairs, 0),
        [whole, shape(R, (NX + 1) * PART, dtype=BF16)],
        part_a,
        arrived_a,
        place,
    )
    wire_a = traded(wire_a, 0, 1)
    part_b, wire_b = call(
        functools.partial(rhs_pairs, 1),
        [whole, shape(R, (NX + 1) * PART, dtype=BF16)],
        part_b,
        arrived_b,
        place,
    )
    wire_b = traded(wire_b, 1, 1)
    pair = [shape(R, HALF + 2 * LANES), shape(R, 2 * LANES)]
    low = shape(R, NX * PART, dtype=BF16)
    rhs_a, lows_a, tang, sums = call(
        first_tangents,
        [shape(R, PART), low, shape(R, N), shape(R, LANES + NB)],
        part_a,
        wire_a,
        examples,
        lamf,
        wfloat,
        onehot,
        place,
        flops=work,
    )
    rhs_b, lows_b, send, rest = call(
        first_tangents_rest,
        [shape(R, PART), low, *pair],
        part_b,
        wire_b,
        examples,
        lamf,
        wfloat,
        onehot,
        tang,
        sums,
        place,
        scratch=[pltpu.VMEM((R, NB), F32)],
        flops=work,
    )
    arrived = summed(lows_b, examples, tang, send, rest, place, work // 2)
    tang_first, weighted, kept_first = call(
        weigh,
        [shape(R, HALF), shape(R, HALF + LANES, dtype=BF16), shape(R, 2 * LANES)],
        arrived,
        curvew,
        place,
    )
    other = swapped(weighted)
    own_a, own_b = call(own_products, [whole, whole], weighted, examples, place, flops=work)
    part_a = call(
        products,
        shape(R, NX * PART + LANES, dtype=BF16),
        own_a,
        other,
        kept_first,
        examples,
        place,
        flops=work,
    )
    arrived_a = traded(part_a, 0, 0)
    part_b = call(
        products_rest,
        shape(R, NX * PART, dtype=BF16),
        own_b,
        other,
        examples,
        place,
        flops=work,
    )
    arrived_b = traded(part_b, 1, 0)
    mine_a = call(
        product_pairs, shape(R, NX * PART + LANES, dtype=BF16), part_a, arrived_a
    )
    other_a = traded(mine_a, 0, 1)
    mine_b = call(product_pairs, shape(R, NX * PART, dtype=BF16), part_b, arrived_b)
    other_b = traded(mine_b, 1, 1)
    resid_a, tang, sums, kept = call(
        second_tangents,
        [shape(R, PART), shape(R, N), shape(R, LANES + NB), shape(R, LANES)],
        mine_a,
        other_a,
        rhs_a,
        lows_a,
        examples,
        lamf,
        wfloat,
        onehot,
        place,
        scratch=[pltpu.VMEM((R, NX * PART), BF16)],
        flops=work,
    )
    resid_b, pieces, send, rest = call(
        second_tangents_rest,
        [shape(R, PART), low, *pair],
        mine_b,
        other_b,
        rhs_b,
        lows_b,
        examples,
        lamf,
        wfloat,
        onehot,
        tang,
        sums,
        kept,
        place,
        scratch=[pltpu.VMEM((R, NB), F32)],
        flops=work,
    )
    arrived = summed(pieces, examples, tang, send, rest, place, work // 2)
    out = call(
        curvature,
        shape(NC * NX, R, LANES),
        arrived,
        curvew,
        tang_first,
        kept_first,
        place,
    )
    arrived = lax.all_to_all(out, ("c", "x"), 0, 0, tiled=True)
    solve, hyper = call(
        finish,
        [shape(R, OWN), shape(1, R)],
        arrived,
        kept,
        rhs_a,
        rhs_b,
        resid_a,
        resid_b,
        strengths,
        place,
    )
    return solve, hyper.reshape(R, 1)


def solution(mesh):
    fine = Mesh(mesh.devices.reshape(NY, NZ, NC, NX), ("y", "z", "c", "x"))
    feat = ("y", "z", "c")
    placed = (P("x", feat), P(feat), P("x"), P("x"), P(None, "x"), P(), P(feat))
    return jax.shard_map(
        shards,
        mesh=fine,
        in_specs=placed,
        out_specs=(P(None, (*feat, "x")), P(None, (*feat, "x"))),
        check_vma=False,
    )
```

```python
import functools

import jax
import jax.numpy as jnp
from jax import lax
from jax.experimental import pallas as pl
from jax.experimental.pallas import tpu as pltpu
from jax.sharding import Mesh
from jax.sharding import PartitionSpec as P

F32 = jnp.float32
BF16 = jnp.bfloat16
NT = (((1,), (1,)), ((), ()))
NY, NZ, NC, NX = 4, 8, 2, 4
R = 32
N = 1024
HALF = N // NC
W = 4096
OWN = W // NX
NB = 256
TOTAL = float(N * NX)
LANES = 128
PART = OWN // 2
VMEM = pl.BlockSpec(memory_space=pltpu.VMEM)
HBM = pl.BlockSpec(memory_space=pltpu.HBM)


def call(body, outs, *arrays, scratch=(), limit=16, hbm=(), flops=0):
    specs = [HBM if i in hbm else VMEM for i in range(len(arrays))]
    arrays = [
        pltpu.with_memory_space_constraint(a, pltpu.HBM) if i in hbm else a
        for i, a in enumerate(arrays)
    ]
    return pl.pallas_call(
        body,
        out_shape=outs,
        in_specs=specs,
        out_specs=jax.tree.map(lambda _: VMEM, outs),
        scratch_shapes=scratch,
        compiler_params=pltpu.CompilerParams(vmem_limit_bytes=limit << 20),
        cost_estimate=pl.CostEstimate(flops=flops, bytes_accessed=4 << 20, transcendentals=0),
    )(*arrays)


def shape(*dims, dtype=F32):
    return jax.ShapeDtypeStruct(dims, dtype)


def lane_ids(lanes=LANES):
    return lax.broadcasted_iota(jnp.int32, (R, lanes), 1)


def column(tile, lane):
    return jnp.sum(jnp.where(lane_ids(tile.shape[1]) == lane, tile, 0.0), axis=1, keepdims=True)


def columns(values, first=0):
    lanes = lane_ids()
    tile = jnp.zeros((R, LANES), F32)
    for i, value in enumerate(values):
        tile = jnp.where(lanes == first + i, value, tile)
    return tile


def terms(value, count):
    found = []
    for _ in range(count):
        term = value.astype(BF16).astype(F32)
        found.append(term)
        value = value - term
    return found


def to_terms(tile):
    first, second, third = terms(tile, 3)
    return first + pltpu.roll(second, 8, 1) + pltpu.roll(third, 16, 1)


def from_terms(tile):
    total = tile + pltpu.roll(tile, LANES - 8, 1) + pltpu.roll(tile, LANES - 16, 1)
    return jnp.where(lane_ids() < 8, total, 0.0)


def chunk(index, size):
    return pl.ds(pl.multiple_of(index * size, size), size)


def block_sums(vec, weight, onehot):
    parts = jnp.concatenate(terms(vec * weight, 3), axis=0).astype(BF16)
    sums = lax.dot_general(parts, onehot, NT, preferred_element_type=F32)
    return sums[:R] + sums[R : 2 * R] + sums[2 * R :]


def prepare(ids, strengths, place, gradw, lamf, onehot):
    kinds = lax.broadcasted_iota(jnp.int32, (NB, OWN), 0)
    rows = lax.broadcasted_iota(jnp.int32, (16, NB), 0)
    split3 = jnp.zeros((16, NB), F32)
    for i, term in enumerate(terms(strengths[...], 3)):
        split3 = jnp.where(rows == i, term, split3)
    split3 = split3.astype(BF16)
    for j in range(NX):
        hot = (kinds == ids[:, j * OWN : (j + 1) * OWN]).astype(F32).astype(BF16)
        found = jnp.dot(split3, hot, preferred_element_type=F32)
        lamf[:, j * OWN : (j + 1) * OWN] = found[0:1] + found[1:2] + found[2:3]
    own = ids[:, chunk(place[0, 3], OWN)]
    core = lax.shift_right_logical(own, 2) & 1
    moved = core * 128 + lax.shift_right_logical(own, 3) * 4 + (own & 3)
    onehot[...] = (kinds == moved).astype(F32).astype(BF16)


def margins(source, given, place, margin, examples, wfloat, weights, arrival):
    width = W // 8

    def fetch(i):
        at = (slice(None), pl.ds(i * width, width))
        return pltpu.make_async_copy(source.at[at], examples.at[at], arrival.at[i])

    small = pltpu.make_async_copy(given, weights, arrival.at[8])
    small.start()
    for i in range(8):
        fetch(i).start()
    small.wait()
    lines = weights[...].astype(F32)
    line = jnp.concatenate([lines[i : i + 1] for i in range(W // LANES)], axis=1)
    wfloat[...] = line
    rhs = jnp.broadcast_to(line, (16, W)).astype(BF16)
    total = None
    for i in range(8):
        fetch(i).wait()
        cols = slice(i * width, (i + 1) * width)
        term = lax.dot_general(
            rhs[:, cols], examples[:, cols], NT, preferred_element_type=F32
        )
        total = term if total is None else total + term
    for i in range(8):
        margin[i : i + 1, :] = total[0:1, i * LANES : (i + 1) * LANES]


def partner(x, which, stage):
    return x ^ (1 if which == stage else 3)


def part_of(owner, which):
    return pl.ds(pl.multiple_of(owner * OWN + which * PART, PART), PART)


def rhs_parts(which, gradw, examples, place, part, wire):
    x = place[0, 3]
    for k in range(NX):
        found = jnp.dot(
            gradw, examples[:, part_of(k, which)], preferred_element_type=F32
        )
        cols = slice(k * PART, (k + 1) * PART)
        part[:, cols] = found
        wire[:, cols] = found.astype(BF16)
    for i, owner in enumerate((partner(x, which, 0), x ^ 2)):
        found = part[:, chunk(owner, PART)]
        rest = found - found.astype(BF16).astype(F32)
        wire[:, (NX + i) * PART : (NX + i + 1) * PART] = rest.astype(BF16)


def gradients(
    margin_parts, labels, split, val_weight, examples, place, part, wire, curvew, gradw
):
    whole = jnp.sum(margin_parts[...], axis=0)
    margin = jnp.concatenate([whole[i : i + 1] for i in range(8)], axis=1)
    prob = 1.0 / (1.0 + jnp.exp(-margin))
    train = split[...].astype(F32)
    curvew[...] = train * prob * (1.0 - prob)
    err = (1.0 - train) * (prob - labels[...].astype(F32))
    found = (val_weight[...] * err / jnp.sqrt(F32(TOTAL))).astype(BF16)
    gradw[...] = found
    rhs_parts(0, found, examples, place, part, wire)


def gradients_rest(gradw, examples, place, part, wire):
    rhs_parts(1, gradw[...], examples, place, part, wire)


def rhs_pairs(which, part, arrived, place, both, wire):
    x = place[0, 3]
    other = partner(x, which, 1)
    both[...] = part[...] + arrived[:, : NX * PART].astype(F32)
    for i, owner in enumerate((x, other)):
        rest = arrived[:, (NX + i) * PART : (NX + i + 1) * PART].astype(F32)
        both[:, chunk(owner, PART)] += rest
    wire[:, : NX * PART] = both[...].astype(BF16)
    found = both[:, chunk(other, PART)]
    wire[:, NX * PART :] = (found - found.astype(BF16).astype(F32)).astype(BF16)


def tangents(pieces, which, examples, before, tang, start, count):
    for i in range(count // 256):
        rows = pl.ds(pl.multiple_of(start + i * 256, 256), 256)
        total = None if before is None else before[:, rows]
        for k in range(NX):
            term = lax.dot_general(
                pieces[:, k * PART : (k + 1) * PART],
                examples[rows, part_of(k, which)],
                NT,
                preferred_element_type=F32,
            )
            total = term if total is None else total + term
        tang[:, i * 256 : (i + 1) * 256] = total


def other_half(pieces, examples, before, scalars, blocks, total, place, send, rest):
    core = place[0, 2]
    tangents(pieces, 1, examples, before, send, (1 - core) * HALF, HALF)
    total[...] = blocks
    send[:, HALF : HALF + LANES] = scalars
    send[:, HALF + LANES :] = total[:, chunk(1 - core, LANES)]
    rest[:, :LANES] = scalars
    rest[:, LANES:] = total[:, chunk(core, LANES)]


def own_half(pieces, examples, before, place, keep):
    tangents(pieces, 1, examples, before, keep, place[0, 2] * HALF, HALF)


def first_part(which, part, wire, lamf, wfloat, onehot, place, rhs, lows):
    x = place[0, 3]
    lows[...] = (part[...] + wire[:, : NX * PART].astype(F32)).astype(BF16)
    cols = chunk(x, PART)
    vec = part[:, cols] + wire[:, cols].astype(F32) + wire[:, NX * PART :].astype(F32)
    rhs[...] = vec
    lows[:, cols] = vec.astype(BF16)
    own = part_of(x, which)
    square = vec * vec
    norm = jnp.sum(square, axis=1, keepdims=True)
    scaled = jnp.sum(lamf[:, own] * square, axis=1, keepdims=True)
    hot = onehot[:, which * PART : (which + 1) * PART]
    blocks = block_sums(vec, wfloat[:, own], hot)
    return columns([norm, scaled]), blocks


def first_tangents(
    part, wire, examples, lamf, wfloat, onehot, place, rhs, lows, tang, sums
):
    scalars, blocks = first_part(0, part, wire, lamf, wfloat, onehot, place, rhs, lows)
    tangents(lows, 0, examples, None, tang, 0, N)
    sums[:, :LANES] = scalars
    sums[:, LANES:] = blocks


def first_tangents_rest(
    part, wire, examples, lamf, wfloat, onehot, before, sums, place,
    rhs, lows, send, rest, total,
):
    scalars, blocks = first_part(1, part, wire, lamf, wfloat, onehot, place, rhs, lows)
    scalars = sums[:, :LANES] + scalars
    blocks = sums[:, LANES:] + blocks
    other_half(lows, examples, before, scalars, blocks, total, place, send, rest)


def to_wire(keep, rest, arrived, place, wire0, wire1, wire2, wire3):
    tang = (keep[...] + arrived[:, :HALF]).astype(BF16)
    scalars = to_terms(rest[:, :LANES] + arrived[:, HALF : HALF + LANES])
    high, low = terms(rest[:, LANES:] + arrived[:, HALF + LANES :], 2)
    lanes = lane_ids()
    for s, wire in enumerate((wire0, wire1, wire2, wire3)):
        first = 32 * ((place[0, 0] + s) % NY)
        at64 = pltpu.roll(high, (64 - first + LANES) % LANES, 1)
        at96 = pltpu.roll(low, (96 - first + LANES) % LANES, 1)
        tile = jnp.where(lanes >= 96, at96, jnp.where(lanes >= 64, at64, scalars))
        wire[:, :HALF] = tang
        wire[:, HALF:] = tile.astype(BF16)


def along_y(wire0, wire1, wire2, wire3, out):
    total = wire0[...].astype(F32)
    for wire in (wire1, wire2, wire3):
        total = total + wire[...].astype(F32)
    tang = total[:, :HALF].astype(BF16)
    tile = total[:, HALF:]
    high, low = terms(tile + pltpu.roll(tile, LANES - 32, 1), 2)
    lanes = lane_ids()
    tile = to_terms(from_terms(tile))
    tile = jnp.where(lanes >= 64, high, tile)
    tile = jnp.where(lanes >= 96, pltpu.roll(low, 32, 1), tile).astype(BF16)
    for i in range(NZ):
        out[i, :, :HALF] = tang
        out[i, :, HALF:] = tile


def along_z(arrived):
    tang = arrived[0, :, :HALF].astype(F32)
    tile = arrived[0, :, HALF:].astype(F32)
    for i in range(1, NZ):
        tang = tang + arrived[i, :, :HALF].astype(F32)
        tile = tile + arrived[i, :, HALF:].astype(F32)
    blocks = pltpu.roll(tile, 64, 1) + pltpu.roll(tile, 32, 1)
    return tang, from_terms(tile), jnp.where(lane_ids() < 32, blocks, 0.0)


def weigh(arrived, curvew, place, tang_out, weighted, kept):
    tang, scalars, blocks = along_z(arrived)
    tang_out[...] = tang
    half = curvew[:, chunk(place[0, 2], HALF)]
    product = half * tang
    weighted[:, :HALF] = product.astype(BF16)
    curv = columns([jnp.sum(product * tang, axis=1, keepdims=True)], 2)
    weighted[:, HALF:] = to_terms(curv).astype(BF16)
    kept[:, :LANES] = scalars + curv
    kept[:, LANES:] = blocks


def own_products(weighted, examples, place, part_a, part_b):
    rows = chunk(place[0, 2], HALF)
    for which, part in enumerate((part_a, part_b)):
        for k in range(NX):
            part[:, k * PART : (k + 1) * PART] = jnp.dot(
                weighted[:, :HALF],
                examples[rows, part_of(k, which)],
                preferred_element_type=F32,
            )


def product_parts(which, mine, other, examples, place, part):
    rows = chunk(1 - place[0, 2], HALF)
    for k in range(NX):
        cols = slice(k * PART, (k + 1) * PART)
        rest = jnp.dot(
            other[:, :HALF], examples[rows, part_of(k, which)], preferred_element_type=F32
        )
        part[:, cols] = (mine[:, cols] + rest).astype(BF16)


def products(mine, other, kept, examples, place, part):
    scalars = kept[:, :LANES] + from_terms(other[:, HALF:].astype(F32))
    part[:, NX * PART :] = to_terms(scalars).astype(BF16)
    product_parts(0, mine, other, examples, place, part)


def products_rest(mine, other, examples, place, part):
    product_parts(1, mine, other, examples, place, part)


def product_pairs(mine, other, wire):
    both = mine[...].astype(F32) + other[...].astype(F32)
    wire[:, : NX * PART] = both[:, : NX * PART].astype(BF16)
    if mine.shape[1] > NX * PART:
        wire[:, NX * PART :] = to_terms(from_terms(both[:, NX * PART :])).astype(BF16)


def second_part(
    which, alpha, mine, other, rhs, lows, lamf, wfloat, onehot, place, resid, pieces
):
    def step(cols, lam, direc):
        total = mine[:, cols].astype(F32) + other[:, cols].astype(F32)
        return direc - alpha * (total / F32(TOTAL) + lam * direc)

    for k in range(NX):
        cols = slice(k * PART, (k + 1) * PART)
        left = step(cols, lamf[:, part_of(k, which)], lows[:, cols].astype(F32))
        pieces[:, cols] = left.astype(BF16)
    x = place[0, 3]
    own = part_of(x, which)
    cols = chunk(x, PART)
    lam = lamf[:, own]
    direc = rhs[...]
    left = step(cols, lam, direc)
    resid[...] = left
    pieces[:, cols] = left.astype(BF16)
    scalars = columns(
        [
            jnp.sum(left * left, axis=1, keepdims=True),
            jnp.sum(lam * left * left, axis=1, keepdims=True),
            jnp.sum(lam * left * direc, axis=1, keepdims=True),
        ]
    )
    hot = onehot[:, which * PART : (which + 1) * PART]
    blocks = block_sums(left, wfloat[:, own], hot)
    return scalars, blocks


def second_tangents(
    mine, other, rhs, lows, examples, lamf, wfloat, onehot, place,
    resid, tang, sums, kept, pieces,
):
    tile = mine[:, NX * PART :].astype(F32) + other[:, NX * PART :].astype(F32)
    tile = from_terms(tile)
    norm, scaled, curv = (column(tile, i) for i in range(3))
    alpha = norm / (curv / F32(TOTAL) + scaled)
    kept[...] = jnp.where(lane_ids() == 3, alpha, tile)
    scalars, blocks = second_part(
        0, alpha, mine, other, rhs, lows, lamf, wfloat, onehot, place, resid, pieces
    )
    tangents(pieces, 0, examples, None, tang, 0, N)
    sums[:, :LANES] = scalars
    sums[:, LANES:] = blocks


def second_tangents_rest(
    mine, other, rhs, lows, examples, lamf, wfloat, onehot, before, sums, kept,
    place, resid, pieces, send, rest, total,
):
    scalars, blocks = second_part(
        1, column(kept[...], 3), mine, other, rhs, lows, lamf, wfloat, onehot, place,
        resid, pieces,
    )
    scalars = sums[:, :LANES] + scalars
    blocks = sums[:, LANES:] + blocks
    other_half(pieces, examples, before, scalars, blocks, total, place, send, rest)


def curvature(arrived, curvew, tang_first, kept, place, out):
    tang, scalars, blocks = along_z(arrived)
    half = curvew[:, chunk(place[0, 2], HALF)]
    product = half * tang
    both = jnp.sum(product * tang, axis=1, keepdims=True)
    cross = jnp.sum(product * tang_first[...], axis=1, keepdims=True)
    tile = jnp.where(lane_ids() < 3, scalars, columns([both, cross], 3))
    lanes = lane_ids()
    shift = 4 * place[0, 1]
    now = pltpu.roll(blocks, (32 - shift + LANES) % LANES, 1)
    before = pltpu.roll(kept[:, LANES:], (36 - shift + LANES) % LANES, 1)
    tile = jnp.where((lanes >= 32) & (lanes < 36), now, tile)
    tile = jnp.where((lanes >= 36) & (lanes < 40), before, tile)
    out[...] = tile


def join(tile, near, core, across, out):
    lanes = lane_ids()
    shared = (lanes == 3) | (lanes == 4)
    total = tile[...] + near[...]
    out[...] = total + jnp.where(shared, core[...] + across[...], 0.0)


def finish(
    tile, far, kept, rhs_a, rhs_b, resid_a, resid_b, strengths, place, solve, hyper
):
    core, x = place[0, 2], place[0, 3]
    mine = tile[...] + far[...]
    first_step = kept[...]
    norm, scaled_first, curv_first, alpha = (column(first_step, i) for i in range(4))
    norm_next, scaled, mixed = (column(mine, i) for i in range(3))
    both, cross = column(mine, 3), column(mine, 4)
    beta = norm_next / norm
    curv = (both + 2.0 * beta * cross + beta * beta * curv_first) / F32(TOTAL)
    curv = curv + (scaled + 2.0 * beta * mixed + beta * beta * scaled_first)
    alpha_next = norm_next / curv
    for i, (rhs, resid) in enumerate(((rhs_a, resid_a), (rhs_b, resid_b))):
        first = rhs[...]
        solve[:, i * PART : (i + 1) * PART] = alpha * first + alpha_next * (
            resid[...] + beta * first
        )
    now, before = column(mine, 32 + x), column(mine, 36 + x)
    block = ((place[0, 0] * NZ + place[0, 1]) * NC + core) * NX + x
    kinds = lax.broadcasted_iota(jnp.int32, (1, NB), 1)
    strength = jnp.sum(jnp.where(kinds == block, strengths[...], 0.0), axis=1, keepdims=True)
    found = -strength * (alpha * before + alpha_next * (now + beta * before))
    hyper[...] = jnp.transpose(jnp.broadcast_to(found, (R, LANES)))[0:1]


def shift(array, axis, length, by):
    return lax.ppermute(array, axis, [(i, (i + by) % length) for i in range(length)])


def traded(array, which, stage):
    return lax.ppermute(array, "x", [(i, partner(i, which, stage)) for i in range(NX)])


def moved(array, core, flip):
    pairs = [(c * NX + x, (c ^ core) * NX + (x ^ flip)) for c in range(NC) for x in range(NX)]
    return lax.ppermute(array, ("c", "x"), pairs)


def swapped(array):
    return lax.ppermute(array, "c", [(0, 1), (1, 0)])


def summed(pieces, examples, before, send, rest, place, flops):
    arrived = swapped(send)
    keep = call(own_half, shape(R, HALF), pieces, examples, before, place, flops=flops)
    line = shape(R, HALF + LANES, dtype=BF16)
    wires = call(to_wire, [line] * NY, keep, rest, arrived, place)
    near = [shift(wires[by], "y", NY, by) for by in (1, NY - 1)]
    far = shift(wires[2], "y", NY, 2)
    out = call(along_y, shape(NZ, R, HALF + LANES, dtype=BF16), wires[0], *near, far)
    return lax.all_to_all(out, "z", 0, 0, tiled=True)


def shards(examples, weights, labels, split, val_weight, strengths, block_ids):
    place = jnp.stack([lax.axis_index(axis) for axis in ("y", "z", "c", "x")])
    place = place.astype(jnp.int32).reshape(1, 4)
    strengths = strengths.reshape(1, NB)
    margin, examples, wfloat = call(
        margins,
        [shape(8, 128), pltpu.VMEM((N, W), BF16), shape(1, W)],
        examples,
        weights.reshape(W // LANES, LANES),
        place,
        scratch=[pltpu.VMEM((W // LANES, LANES), BF16), pltpu.SemaphoreType.DMA((9,))],
        hbm=(0, 1),
    )
    margin = margin + swapped(margin)
    margin_parts = lax.all_to_all(
        jnp.broadcast_to(margin[None], (NY * NZ, 8, 128)), ("y", "z"), 0, 0, tiled=True
    )
    work = 2 * R * N * W // 2
    whole = shape(R, NX * PART)
    part_a, wire_a, curvew, gradw = call(
        gradients,
        [
            whole,
            shape(R, (NX + 2) * PART, dtype=BF16),
            shape(1, N),
            shape(R, N, dtype=BF16),
        ],
        margin_parts,
        labels.reshape(1, N),
        split.reshape(1, N),
        val_weight,
        examples,
        place,
        flops=work,
    )
    arrived_a = traded(wire_a, 0, 0)
    part_b, wire_b = call(
        gradients_rest,
        [whole, shape(R, (NX + 2) * PART, dtype=BF16)],
        gradw,
        examples,
        place,
        flops=work,
    )
    arrived_b = traded(wire_b, 1, 0)
    lamf, onehot = call(
        prepare,
        [shape(1, W), shape(NB, OWN, dtype=BF16)],
        block_ids.reshape(1, W),
        strengths,
        place,
        gradw,
    )
    part_a, wire_a = call(
        functools.partial(rhs_pairs, 0),
        [whole, shape(R, (NX + 1) * PART, dtype=BF16)],
        part_a,
        arrived_a,
        place,
    )
    wire_a = traded(wire_a, 0, 1)
    part_b, wire_b = call(
        functools.partial(rhs_pairs, 1),
        [whole, shape(R, (NX + 1) * PART, dtype=BF16)],
        part_b,
        arrived_b,
        place,
    )
    wire_b = traded(wire_b, 1, 1)
    pair = [shape(R, HALF + 2 * LANES), shape(R, 2 * LANES)]
    low = shape(R, NX * PART, dtype=BF16)
    rhs_a, lows_a, tang, sums = call(
        first_tangents,
        [shape(R, PART), low, shape(R, N), shape(R, LANES + NB)],
        part_a,
        wire_a,
        examples,
        lamf,
        wfloat,
        onehot,
        place,
        flops=work,
    )
    rhs_b, lows_b, send, rest = call(
        first_tangents_rest,
        [shape(R, PART), low, *pair],
        part_b,
        wire_b,
        examples,
        lamf,
        wfloat,
        onehot,
        tang,
        sums,
        place,
        scratch=[pltpu.VMEM((R, NB), F32)],
        flops=work,
    )
    arrived = summed(lows_b, examples, tang, send, rest, place, work // 2)
    tang_first, weighted, kept_first = call(
        weigh,
        [shape(R, HALF), shape(R, HALF + LANES, dtype=BF16), shape(R, 2 * LANES)],
        arrived,
        curvew,
        place,
    )
    other = swapped(weighted)
    own_a, own_b = call(own_products, [whole, whole], weighted, examples, place, flops=work)
    part_a = call(
        products,
        shape(R, NX * PART + LANES, dtype=BF16),
        own_a,
        other,
        kept_first,
        examples,
        place,
        flops=work,
    )
    arrived_a = traded(part_a, 0, 0)
    part_b = call(
        products_rest,
        shape(R, NX * PART, dtype=BF16),
        own_b,
        other,
        examples,
        place,
        flops=work,
    )
    arrived_b = traded(part_b, 1, 0)
    mine_a = call(
        product_pairs, shape(R, NX * PART + LANES, dtype=BF16), part_a, arrived_a
    )
    other_a = traded(mine_a, 0, 1)
    mine_b = call(product_pairs, shape(R, NX * PART, dtype=BF16), part_b, arrived_b)
    other_b = traded(mine_b, 1, 1)
    resid_a, tang, sums, kept = call(
        second_tangents,
        [shape(R, PART), shape(R, N), shape(R, LANES + NB), shape(R, LANES)],
        mine_a,
        other_a,
        rhs_a,
        lows_a,
        examples,
        lamf,
        wfloat,
        onehot,
        place,
        scratch=[pltpu.VMEM((R, NX * PART), BF16)],
        flops=work,
    )
    resid_b, pieces, send, rest = call(
        second_tangents_rest,
        [shape(R, PART), low, *pair],
        mine_b,
        other_b,
        rhs_b,
        lows_b,
        examples,
        lamf,
        wfloat,
        onehot,
        tang,
        sums,
        kept,
        place,
        scratch=[pltpu.VMEM((R, NB), F32)],
        flops=work,
    )
    arrived = summed(pieces, examples, tang, send, rest, place, work // 2)
    tile = call(
        curvature,
        shape(R, LANES),
        arrived,
        curvew,
        tang_first,
        kept_first,
        place,
    )
    others = [moved(tile, core, flip) for core, flip in ((0, 1), (1, 0), (1, 1))]
    tile = call(join, shape(R, LANES), tile, *others)
    far = moved(tile, 0, 3)
    solve, hyper = call(
        finish,
        [shape(R, OWN), shape(1, R)],
        tile,
        far,
        kept,
        rhs_a,
        rhs_b,
        resid_a,
        resid_b,
        strengths,
        place,
    )
    return solve, hyper.reshape(R, 1)


def solution(mesh):
    fine = Mesh(mesh.devices.reshape(NY, NZ, NC, NX), ("y", "z", "c", "x"))
    feat = ("y", "z", "c")
    placed = (P("x", feat), P(feat), P("x"), P("x"), P(None, "x"), P(), P(feat))
    return jax.shard_map(
        shards,
        mesh=fine,
        in_specs=placed,
        out_specs=(P(None, (*feat, "x")), P(None, (*feat, "x"))),
        check_vma=False,
    )
```

```python
import functools

import jax
import jax.numpy as jnp
from jax import lax
from jax.experimental import pallas as pl
from jax.experimental.pallas import tpu as pltpu
from jax.sharding import Mesh
from jax.sharding import PartitionSpec as P

F32 = jnp.float32
BF16 = jnp.bfloat16
NT = (((1,), (1,)), ((), ()))
NY, NZ, NC, NX = 4, 8, 2, 4
R = 32
N = 1024
HALF = N // NC
W = 4096
OWN = W // NX
NB = 256
TOTAL = float(N * NX)
LANES = 128
PART = OWN // 2
VMEM = pl.BlockSpec(memory_space=pltpu.VMEM)
HBM = pl.BlockSpec(memory_space=pltpu.HBM)


def call(body, outs, *arrays, scratch=(), limit=16, hbm=(), flops=0):
    specs = [HBM if i in hbm else VMEM for i in range(len(arrays))]
    arrays = [
        pltpu.with_memory_space_constraint(a, pltpu.HBM) if i in hbm else a
        for i, a in enumerate(arrays)
    ]
    return pl.pallas_call(
        body,
        out_shape=outs,
        in_specs=specs,
        out_specs=jax.tree.map(lambda _: VMEM, outs),
        scratch_shapes=scratch,
        compiler_params=pltpu.CompilerParams(vmem_limit_bytes=limit << 20),
        cost_estimate=pl.CostEstimate(flops=flops, bytes_accessed=4 << 20, transcendentals=0),
    )(*arrays)


def shape(*dims, dtype=F32):
    return jax.ShapeDtypeStruct(dims, dtype)


def lane_ids(lanes=LANES):
    return lax.broadcasted_iota(jnp.int32, (R, lanes), 1)


def column(tile, lane):
    return jnp.sum(jnp.where(lane_ids(tile.shape[1]) == lane, tile, 0.0), axis=1, keepdims=True)


def columns(values, first=0):
    lanes = lane_ids()
    tile = jnp.zeros((R, LANES), F32)
    for i, value in enumerate(values):
        tile = jnp.where(lanes == first + i, value, tile)
    return tile


def terms(value, count):
    found = []
    for _ in range(count):
        term = value.astype(BF16).astype(F32)
        found.append(term)
        value = value - term
    return found


def to_terms(tile):
    first, second, third = terms(tile, 3)
    return first + pltpu.roll(second, 8, 1) + pltpu.roll(third, 16, 1)


def from_terms(tile):
    total = tile + pltpu.roll(tile, LANES - 8, 1) + pltpu.roll(tile, LANES - 16, 1)
    return jnp.where(lane_ids() < 8, total, 0.0)


def chunk(index, size):
    return pl.ds(pl.multiple_of(index * size, size), size)


def block_sums(vec, weight, onehot):
    parts = jnp.concatenate(terms(vec * weight, 3), axis=0).astype(BF16)
    sums = lax.dot_general(parts, onehot, NT, preferred_element_type=F32)
    return sums[:R] + sums[R : 2 * R] + sums[2 * R :]


def prepare(ids, strengths, place, gradw, lamf, onehot):
    kinds = lax.broadcasted_iota(jnp.int32, (NB, OWN), 0)
    rows = lax.broadcasted_iota(jnp.int32, (16, NB), 0)
    split3 = jnp.zeros((16, NB), F32)
    for i, term in enumerate(terms(strengths[...], 3)):
        split3 = jnp.where(rows == i, term, split3)
    split3 = split3.astype(BF16)
    for j in range(NX):
        hot = (kinds == ids[:, j * OWN : (j + 1) * OWN]).astype(F32).astype(BF16)
        found = jnp.dot(split3, hot, preferred_element_type=F32)
        lamf[:, j * OWN : (j + 1) * OWN] = found[0:1] + found[1:2] + found[2:3]
    own = ids[:, chunk(place[0, 3], OWN)]
    core = lax.shift_right_logical(own, 2) & 1
    moved = core * 128 + lax.shift_right_logical(own, 3) * 4 + (own & 3)
    onehot[...] = (kinds == moved).astype(F32).astype(BF16)


def margins(source, given, place, margin, examples, wfloat, weights, arrival):
    width = W // 8

    def fetch(i):
        at = (slice(None), pl.ds(i * width, width))
        return pltpu.make_async_copy(source.at[at], examples.at[at], arrival.at[i])

    small = pltpu.make_async_copy(given, weights, arrival.at[8])
    small.start()
    for i in range(8):
        fetch(i).start()
    small.wait()
    lines = weights[...].astype(F32)
    line = jnp.concatenate([lines[i : i + 1] for i in range(W // LANES)], axis=1)
    wfloat[...] = line
    rhs = jnp.broadcast_to(line, (16, W)).astype(BF16)
    total = None
    for i in range(8):
        fetch(i).wait()
        cols = slice(i * width, (i + 1) * width)
        term = lax.dot_general(
            rhs[:, cols], examples[:, cols], NT, preferred_element_type=F32
        )
        total = term if total is None else total + term
    for i in range(8):
        margin[i : i + 1, :] = total[0:1, i * LANES : (i + 1) * LANES]


def partner(x, which, stage):
    return x ^ (1 if which == stage else 3)


def part_of(owner, which):
    return pl.ds(pl.multiple_of(owner * OWN + which * PART, PART), PART)


def rhs_parts(which, gradw, examples, place, part, wire):
    x = place[0, 3]
    for k in range(NX):
        found = jnp.dot(
            gradw, examples[:, part_of(k, which)], preferred_element_type=F32
        )
        cols = slice(k * PART, (k + 1) * PART)
        part[:, cols] = found
        wire[:, cols] = found.astype(BF16)
    for i, owner in enumerate((partner(x, which, 0), x ^ 2)):
        found = part[:, chunk(owner, PART)]
        rest = found - found.astype(BF16).astype(F32)
        wire[:, (NX + i) * PART : (NX + i + 1) * PART] = rest.astype(BF16)


def gradients(
    margin_parts, labels, split, val_weight, examples, place, part, wire, curvew, gradw
):
    whole = jnp.sum(margin_parts[...], axis=0)
    margin = jnp.concatenate([whole[i : i + 1] for i in range(8)], axis=1)
    prob = 1.0 / (1.0 + jnp.exp(-margin))
    train = split[...].astype(F32)
    curvew[...] = train * prob * (1.0 - prob)
    err = (1.0 - train) * (prob - labels[...].astype(F32))
    found = (val_weight[...] * err / jnp.sqrt(F32(TOTAL))).astype(BF16)
    gradw[...] = found
    rhs_parts(0, found, examples, place, part, wire)


def gradients_rest(gradw, examples, place, part, wire):
    rhs_parts(1, gradw[...], examples, place, part, wire)


def rhs_pairs(which, part, arrived, place, both, wire):
    x = place[0, 3]
    other = partner(x, which, 1)
    both[...] = part[...] + arrived[:, : NX * PART].astype(F32)
    for i, owner in enumerate((x, other)):
        rest = arrived[:, (NX + i) * PART : (NX + i + 1) * PART].astype(F32)
        both[:, chunk(owner, PART)] += rest
    wire[:, : NX * PART] = both[...].astype(BF16)
    found = both[:, chunk(other, PART)]
    wire[:, NX * PART :] = (found - found.astype(BF16).astype(F32)).astype(BF16)


def tangents(pieces, which, examples, before, tang, start, count):
    for i in range(count // 256):
        rows = pl.ds(pl.multiple_of(start + i * 256, 256), 256)
        total = None if before is None else before[:, rows]
        for k in range(NX):
            term = lax.dot_general(
                pieces[:, k * PART : (k + 1) * PART],
                examples[rows, part_of(k, which)],
                NT,
                preferred_element_type=F32,
            )
            total = term if total is None else total + term
        tang[:, i * 256 : (i + 1) * 256] = total


def other_half(pieces, examples, before, scalars, blocks, total, place, send, rest):
    core = place[0, 2]
    tangents(pieces, 1, examples, before, send, (1 - core) * HALF, HALF)
    total[...] = blocks
    send[:, HALF : HALF + LANES] = scalars
    send[:, HALF + LANES :] = total[:, chunk(1 - core, LANES)]
    rest[:, :LANES] = scalars
    rest[:, LANES:] = total[:, chunk(core, LANES)]


def own_half(pieces, examples, before, place, keep):
    tangents(pieces, 1, examples, before, keep, place[0, 2] * HALF, HALF)


def first_part(which, part, wire, lamf, wfloat, onehot, place, rhs, lows):
    x = place[0, 3]
    lows[...] = (part[...] + wire[:, : NX * PART].astype(F32)).astype(BF16)
    cols = chunk(x, PART)
    vec = part[:, cols] + wire[:, cols].astype(F32) + wire[:, NX * PART :].astype(F32)
    rhs[...] = vec
    lows[:, cols] = vec.astype(BF16)
    own = part_of(x, which)
    square = vec * vec
    norm = jnp.sum(square, axis=1, keepdims=True)
    scaled = jnp.sum(lamf[:, own] * square, axis=1, keepdims=True)
    hot = onehot[:, which * PART : (which + 1) * PART]
    blocks = block_sums(vec, wfloat[:, own], hot)
    return columns([norm, scaled]), blocks


def first_tangents(
    part, wire, examples, lamf, wfloat, onehot, place, rhs, lows, tang, sums
):
    scalars, blocks = first_part(0, part, wire, lamf, wfloat, onehot, place, rhs, lows)
    tangents(lows, 0, examples, None, tang, 0, N)
    sums[:, :LANES] = scalars
    sums[:, LANES:] = blocks


def first_tangents_rest(
    part, wire, examples, lamf, wfloat, onehot, before, sums, place,
    rhs, lows, send, rest, total,
):
    scalars, blocks = first_part(1, part, wire, lamf, wfloat, onehot, place, rhs, lows)
    scalars = sums[:, :LANES] + scalars
    blocks = sums[:, LANES:] + blocks
    other_half(lows, examples, before, scalars, blocks, total, place, send, rest)


def to_wire(keep, rest, arrived, place, wire0, wire1, wire2, wire3):
    tang = (keep[...] + arrived[:, :HALF]).astype(BF16)
    scalars = to_terms(rest[:, :LANES] + arrived[:, HALF : HALF + LANES])
    high, low = terms(rest[:, LANES:] + arrived[:, HALF + LANES :], 2)
    lanes = lane_ids()
    for s, wire in enumerate((wire0, wire1, wire2, wire3)):
        first = 32 * ((place[0, 0] + s) % NY)
        at64 = pltpu.roll(high, (64 - first + LANES) % LANES, 1)
        at96 = pltpu.roll(low, (96 - first + LANES) % LANES, 1)
        tile = jnp.where(lanes >= 96, at96, jnp.where(lanes >= 64, at64, scalars))
        wire[:, :HALF] = tang
        wire[:, HALF:] = tile.astype(BF16)


def along_y(wire0, wire1, wire2, wire3, out):
    total = wire0[...].astype(F32)
    for wire in (wire1, wire2, wire3):
        total = total + wire[...].astype(F32)
    tang = total[:, :HALF].astype(BF16)
    tile = total[:, HALF:]
    high, low = terms(tile + pltpu.roll(tile, LANES - 32, 1), 2)
    lanes = lane_ids()
    tile = to_terms(from_terms(tile))
    tile = jnp.where(lanes >= 64, high, tile)
    tile = jnp.where(lanes >= 96, pltpu.roll(low, 32, 1), tile).astype(BF16)
    for i in range(NZ):
        out[i, :, :HALF] = tang
        out[i, :, HALF:] = tile


def along_z(arrived):
    tang = arrived[0, :, :HALF].astype(F32)
    tile = arrived[0, :, HALF:].astype(F32)
    for i in range(1, NZ):
        tang = tang + arrived[i, :, :HALF].astype(F32)
        tile = tile + arrived[i, :, HALF:].astype(F32)
    blocks = pltpu.roll(tile, 64, 1) + pltpu.roll(tile, 32, 1)
    return tang, from_terms(tile), jnp.where(lane_ids() < 32, blocks, 0.0)


def weigh(arrived, curvew, place, tang_out, weighted, kept):
    tang, scalars, blocks = along_z(arrived)
    tang_out[...] = tang
    half = curvew[:, chunk(place[0, 2], HALF)]
    product = half * tang
    weighted[:, :HALF] = product.astype(BF16)
    curv = columns([jnp.sum(product * tang, axis=1, keepdims=True)], 2)
    weighted[:, HALF:] = to_terms(curv).astype(BF16)
    kept[:, :LANES] = scalars + curv
    kept[:, LANES:] = blocks


def own_products(weighted, examples, place, part_a, part_b):
    rows = chunk(place[0, 2], HALF)
    for which, part in enumerate((part_a, part_b)):
        for k in range(NX):
            part[:, k * PART : (k + 1) * PART] = jnp.dot(
                weighted[:, :HALF],
                examples[rows, part_of(k, which)],
                preferred_element_type=F32,
            )


def product_parts(which, mine, other, examples, place, part):
    rows = chunk(1 - place[0, 2], HALF)
    for k in range(NX):
        cols = slice(k * PART, (k + 1) * PART)
        rest = jnp.dot(
            other[:, :HALF], examples[rows, part_of(k, which)], preferred_element_type=F32
        )
        part[:, cols] = (mine[:, cols] + rest).astype(BF16)


def products(mine, other, kept, examples, place, part):
    scalars = kept[:, :LANES] + from_terms(other[:, HALF:].astype(F32))
    part[:, NX * PART :] = to_terms(scalars).astype(BF16)
    product_parts(0, mine, other, examples, place, part)


def products_rest(mine, other, examples, place, part):
    product_parts(1, mine, other, examples, place, part)


def product_pairs(mine, other, wire):
    both = mine[...].astype(F32) + other[...].astype(F32)
    wire[:, : NX * PART] = both[:, : NX * PART].astype(BF16)
    if mine.shape[1] > NX * PART:
        wire[:, NX * PART :] = to_terms(from_terms(both[:, NX * PART :])).astype(BF16)


def second_part(
    which, alpha, mine, other, rhs, lows, lamf, wfloat, onehot, place, resid, pieces
):
    def step(cols, lam, direc):
        total = mine[:, cols].astype(F32) + other[:, cols].astype(F32)
        return direc - alpha * (total / F32(TOTAL) + lam * direc)

    for k in range(NX):
        cols = slice(k * PART, (k + 1) * PART)
        left = step(cols, lamf[:, part_of(k, which)], lows[:, cols].astype(F32))
        pieces[:, cols] = left.astype(BF16)
    x = place[0, 3]
    own = part_of(x, which)
    cols = chunk(x, PART)
    lam = lamf[:, own]
    direc = rhs[...]
    left = step(cols, lam, direc)
    resid[...] = left
    pieces[:, cols] = left.astype(BF16)
    scalars = columns(
        [
            jnp.sum(left * left, axis=1, keepdims=True),
            jnp.sum(lam * left * left, axis=1, keepdims=True),
            jnp.sum(lam * left * direc, axis=1, keepdims=True),
        ]
    )
    hot = onehot[:, which * PART : (which + 1) * PART]
    blocks = block_sums(left, wfloat[:, own], hot)
    return scalars, blocks


def second_tangents(
    mine, other, rhs, lows, examples, lamf, wfloat, onehot, place,
    resid, tang, sums, kept, pieces,
):
    tile = mine[:, NX * PART :].astype(F32) + other[:, NX * PART :].astype(F32)
    tile = from_terms(tile)
    norm, scaled, curv = (column(tile, i) for i in range(3))
    alpha = norm / (curv / F32(TOTAL) + scaled)
    kept[...] = jnp.where(lane_ids() == 3, alpha, tile)
    scalars, blocks = second_part(
        0, alpha, mine, other, rhs, lows, lamf, wfloat, onehot, place, resid, pieces
    )
    tangents(pieces, 0, examples, None, tang, 0, N)
    sums[:, :LANES] = scalars
    sums[:, LANES:] = blocks


def second_tangents_rest(
    mine, other, rhs, lows, examples, lamf, wfloat, onehot, before, sums, kept,
    place, resid, pieces, send, rest, total,
):
    scalars, blocks = second_part(
        1, column(kept[...], 3), mine, other, rhs, lows, lamf, wfloat, onehot, place,
        resid, pieces,
    )
    scalars = sums[:, :LANES] + scalars
    blocks = sums[:, LANES:] + blocks
    other_half(pieces, examples, before, scalars, blocks, total, place, send, rest)


def curvature(arrived, curvew, tang_first, kept, place, out):
    tang, scalars, blocks = along_z(arrived)
    half = curvew[:, chunk(place[0, 2], HALF)]
    product = half * tang
    both = jnp.sum(product * tang, axis=1, keepdims=True)
    cross = jnp.sum(product * tang_first[...], axis=1, keepdims=True)
    tile = jnp.where(lane_ids() < 3, scalars, columns([both, cross], 3))
    lanes = lane_ids()
    shift = 4 * place[0, 1]
    now = pltpu.roll(blocks, (32 - shift + LANES) % LANES, 1)
    before = pltpu.roll(kept[:, LANES:], (36 - shift + LANES) % LANES, 1)
    tile = jnp.where((lanes >= 32) & (lanes < 36), now, tile)
    tile = jnp.where((lanes >= 36) & (lanes < 40), before, tile)
    out[...] = tile


def join(tile, near, core, across, out):
    lanes = lane_ids()
    shared = (lanes == 3) | (lanes == 4)
    total = tile[...] + near[...]
    out[...] = total + jnp.where(shared, core[...] + across[...], 0.0)


def finish(
    tile, far, kept, rhs_a, rhs_b, resid_a, resid_b, strengths, place, solve, hyper
):
    core, x = place[0, 2], place[0, 3]
    mine = tile[...] + far[...]
    first_step = kept[...]
    norm, scaled_first, curv_first, alpha = (column(first_step, i) for i in range(4))
    norm_next, scaled, mixed = (column(mine, i) for i in range(3))
    both, cross = column(mine, 3), column(mine, 4)
    beta = norm_next / norm
    curv = (both + 2.0 * beta * cross + beta * beta * curv_first) / F32(TOTAL)
    curv = curv + (scaled + 2.0 * beta * mixed + beta * beta * scaled_first)
    alpha_next = norm_next / curv
    for i, (rhs, resid) in enumerate(((rhs_a, resid_a), (rhs_b, resid_b))):
        first = rhs[...]
        solve[:, i * PART : (i + 1) * PART] = alpha * first + alpha_next * (
            resid[...] + beta * first
        )
    now, before = column(mine, 32 + x), column(mine, 36 + x)
    block = ((place[0, 0] * NZ + place[0, 1]) * NC + core) * NX + x
    kinds = lax.broadcasted_iota(jnp.int32, (1, NB), 1)
    strength = jnp.sum(jnp.where(kinds == block, strengths[...], 0.0), axis=1, keepdims=True)
    found = -strength * (alpha * before + alpha_next * (now + beta * before))
    hyper[...] = jnp.transpose(jnp.broadcast_to(found, (R, LANES)))[0:1]


def shift(array, axis, length, by):
    return lax.ppermute(array, axis, [(i, (i + by) % length) for i in range(length)])


def traded(array, which, stage):
    return lax.ppermute(array, "x", [(i, partner(i, which, stage)) for i in range(NX)])


def moved(array, core, flip):
    pairs = [(c * NX + x, (c ^ core) * NX + (x ^ flip)) for c in range(NC) for x in range(NX)]
    return lax.ppermute(array, ("c", "x"), pairs)


def swapped(array):
    return lax.ppermute(array, "c", [(0, 1), (1, 0)])


def summed(pieces, examples, before, send, rest, place, flops):
    arrived = swapped(send)
    keep = call(own_half, shape(R, HALF), pieces, examples, before, place, flops=flops)
    line = shape(R, HALF + LANES, dtype=BF16)
    wires = call(to_wire, [line] * NY, keep, rest, arrived, place)
    near = [shift(wires[by], "y", NY, by) for by in (1, NY - 1)]
    far = shift(wires[2], "y", NY, 2)
    out = call(along_y, shape(NZ, R, HALF + LANES, dtype=BF16), wires[0], far, *near)
    return lax.all_to_all(out, "z", 0, 0, tiled=True)


def shards(examples, weights, labels, split, val_weight, strengths, block_ids):
    place = jnp.stack([lax.axis_index(axis) for axis in ("y", "z", "c", "x")])
    place = place.astype(jnp.int32).reshape(1, 4)
    strengths = strengths.reshape(1, NB)
    margin, examples, wfloat = call(
        margins,
        [shape(8, 128), pltpu.VMEM((N, W), BF16), shape(1, W)],
        examples,
        weights.reshape(W // LANES, LANES),
        place,
        scratch=[pltpu.VMEM((W // LANES, LANES), BF16), pltpu.SemaphoreType.DMA((9,))],
        hbm=(0, 1),
    )
    margin = margin + swapped(margin)
    margin_parts = lax.all_to_all(
        jnp.broadcast_to(margin[None], (NY * NZ, 8, 128)), ("y", "z"), 0, 0, tiled=True
    )
    work = 2 * R * N * W // 2
    whole = shape(R, NX * PART)
    part_a, wire_a, curvew, gradw = call(
        gradients,
        [
            whole,
            shape(R, (NX + 2) * PART, dtype=BF16),
            shape(1, N),
            shape(R, N, dtype=BF16),
        ],
        margin_parts,
        labels.reshape(1, N),
        split.reshape(1, N),
        val_weight,
        examples,
        place,
        flops=work,
    )
    arrived_a = traded(wire_a, 0, 0)
    part_b, wire_b = call(
        gradients_rest,
        [whole, shape(R, (NX + 2) * PART, dtype=BF16)],
        gradw,
        examples,
        place,
        flops=work,
    )
    arrived_b = traded(wire_b, 1, 0)
    lamf, onehot = call(
        prepare,
        [shape(1, W), shape(NB, OWN, dtype=BF16)],
        block_ids.reshape(1, W),
        strengths,
        place,
        gradw,
    )
    part_a, wire_a = call(
        functools.partial(rhs_pairs, 0),
        [whole, shape(R, (NX + 1) * PART, dtype=BF16)],
        part_a,
        arrived_a,
        place,
    )
    wire_a = traded(wire_a, 0, 1)
    part_b, wire_b = call(
        functools.partial(rhs_pairs, 1),
        [whole, shape(R, (NX + 1) * PART, dtype=BF16)],
        part_b,
        arrived_b,
        place,
    )
    wire_b = traded(wire_b, 1, 1)
    pair = [shape(R, HALF + 2 * LANES), shape(R, 2 * LANES)]
    low = shape(R, NX * PART, dtype=BF16)
    rhs_a, lows_a, tang, sums = call(
        first_tangents,
        [shape(R, PART), low, shape(R, N), shape(R, LANES + NB)],
        part_a,
        wire_a,
        examples,
        lamf,
        wfloat,
        onehot,
        place,
        flops=work,
    )
    rhs_b, lows_b, send, rest = call(
        first_tangents_rest,
        [shape(R, PART), low, *pair],
        part_b,
        wire_b,
        examples,
        lamf,
        wfloat,
        onehot,
        tang,
        sums,
        place,
        scratch=[pltpu.VMEM((R, NB), F32)],
        flops=work,
    )
    arrived = summed(lows_b, examples, tang, send, rest, place, work // 2)
    tang_first, weighted, kept_first = call(
        weigh,
        [shape(R, HALF), shape(R, HALF + LANES, dtype=BF16), shape(R, 2 * LANES)],
        arrived,
        curvew,
        place,
    )
    other = swapped(weighted)
    own_a, own_b = call(own_products, [whole, whole], weighted, examples, place, flops=work)
    part_a = call(
        products,
        shape(R, NX * PART + LANES, dtype=BF16),
        own_a,
        other,
        kept_first,
        examples,
        place,
        flops=work,
    )
    arrived_a = traded(part_a, 0, 0)
    part_b = call(
        products_rest,
        shape(R, NX * PART, dtype=BF16),
        own_b,
        other,
        examples,
        place,
        flops=work,
    )
    arrived_b = traded(part_b, 1, 0)
    mine_a = call(
        product_pairs, shape(R, NX * PART + LANES, dtype=BF16), part_a, arrived_a
    )
    other_a = traded(mine_a, 0, 1)
    mine_b = call(product_pairs, shape(R, NX * PART, dtype=BF16), part_b, arrived_b)
    other_b = traded(mine_b, 1, 1)
    resid_a, tang, sums, kept = call(
        second_tangents,
        [shape(R, PART), shape(R, N), shape(R, LANES + NB), shape(R, LANES)],
        mine_a,
        other_a,
        rhs_a,
        lows_a,
        examples,
        lamf,
        wfloat,
        onehot,
        place,
        scratch=[pltpu.VMEM((R, NX * PART), BF16)],
        flops=work,
    )
    resid_b, pieces, send, rest = call(
        second_tangents_rest,
        [shape(R, PART), low, *pair],
        mine_b,
        other_b,
        rhs_b,
        lows_b,
        examples,
        lamf,
        wfloat,
        onehot,
        tang,
        sums,
        kept,
        place,
        scratch=[pltpu.VMEM((R, NB), F32)],
        flops=work,
    )
    arrived = summed(pieces, examples, tang, send, rest, place, work // 2)
    tile = call(
        curvature,
        shape(R, LANES),
        arrived,
        curvew,
        tang_first,
        kept_first,
        place,
    )
    others = [moved(tile, core, flip) for core, flip in ((0, 1), (1, 0), (1, 1))]
    tile = call(join, shape(R, LANES), tile, *others)
    far = moved(tile, 0, 3)
    solve, hyper = call(
        finish,
        [shape(R, OWN), shape(1, R)],
        tile,
        far,
        kept,
        rhs_a,
        rhs_b,
        resid_a,
        resid_b,
        strengths,
        place,
    )
    return solve, hyper.reshape(R, 1)


def solution(mesh):
    fine = Mesh(mesh.devices.reshape(NY, NZ, NC, NX), ("y", "z", "c", "x"))
    feat = ("y", "z", "c")
    placed = (P("x", feat), P(feat), P("x"), P("x"), P(None, "x"), P(), P(feat))
    return jax.shard_map(
        shards,
        mesh=fine,
        in_specs=placed,
        out_specs=(P(None, (*feat, "x")), P(None, (*feat, "x"))),
        check_vma=False,
    )
```
